256 devices in a mesh: dp: 4 (over x), section: 8 (over z_lo, core), tensor: 8 (over z_hi, y).
Axes of the slice: x: 4, y: 4, z: 8 (z_hi: 2, z_lo: 4; z = z_hi * 4 + z_lo), core: 2. Of those that a mesh axis runs over, the one named last changes fastest.
Arguments:
- states: bfloat16 [16, 512, 8192], P('section', 'dp', 'tensor'), may hold values from -6 to 6
- final_state: bfloat16 [512, 8192], P('dp', 'tensor'), may hold values from -6 to 6
- retained: int32 [8], replicated, may hold values from 0 to 15, as said below
- block_slot: int32 [8], replicated, may hold values from 0 to 7, each once
- w_in: bfloat16 [8, 8192, 4096], P('section', 'tensor', 'dp'), may hold values from -0.0625 to 0.0625
- w_side: bfloat16 [8, 8192, 192], P('section', 'tensor'), may hold values from -0.0234375 to 0.0234375
- w_out: bfloat16 [8, 4096, 8192], P('section', 'dp', 'tensor'), may hold values from -0.09375 to 0.09375
- a_rate: float32 [8, 64], P('section'), may hold values from 0.005 to 0.5
- dt_bias: float32 [8, 64], P('section'), may hold values from -1 to 1
- skip: float32 [8, 64], P('section'), may hold values from -1 to 1
Outputs:
- grad_in: bfloat16 [8, 8192, 4096], P('section', 'tensor', 'dp')
- grad_side: bfloat16 [8, 8192, 192], P('section', 'tensor')
- grad_out: bfloat16 [8, 4096, 8192], P('section', 'dp', 'tensor')
- mean_loss: float32 [8], P('section')
The draws below stay inside these ranges and needn't reach their ends.
Inputs may be any that keep to these rules, and one draw needn't show every extreme that they name: Distinct layers; layer 0 and layer 15 are always retained.
All inputs are finite; a program needn't handle non-finite values.
Results may differ from the reference program's by a relative error of at most 0.0075.
Values may be sent and summed in bfloat16 or wider, within the bound.
A program may use at most 64 MiB of HBM per device.

```python
import math
import jax
import jax.numpy as jnp
from jax import lax

D = 8192
P_SIZE = 64
NS = 64
DI = 4096
HEADS = 64
LAYERS = 16
BLOCKS = 8
TOKENS = 512
N_DP = 4


def draw_retained(key, part):
    key = jax.random.fold_in(key, 11)
    middle = jax.random.permutation(key, LAYERS - 2).astype(jnp.int32) + 1
    ends = jnp.array([0, LAYERS - 1], dtype=jnp.int32)
    picked = jnp.concatenate([ends, middle[:BLOCKS - 2]])
    shuffle = jax.random.permutation(jax.random.fold_in(key, 1), BLOCKS)
    return picked[shuffle].astype(jnp.int32)


def steps_of(rng, dims, split, low, high):
    def one(position, shards_of):
        heights = jax.random.uniform(jax.random.fold_in(jax.random.fold_in(rng, 6), position), (shards_of,), jnp.float32, low / len(split), high / len(split))
        return jnp.repeat(jnp.exp(heights), dims[position] // shards_of).reshape((-1,) + (1,) * (len(dims) - position - 1))

    loudness = one(*split[0])
    for cut in split[1:]:
        loudness = loudness * one(*cut)
    return loudness


def scatter_about(key, dims, spread, limit, cuts=(), kind=jnp.bfloat16):
    drawn = spread * jax.random.normal(key, dims, jnp.float32)
    if cuts:
        drawn = drawn * steps_of(key, dims, cuts, -0.22, 0.18)
    return jnp.clip(drawn, -limit, limit).astype(kind)


def setup_inputs(seed: int = 0) -> dict:
    splits = jax.random.split(jax.random.key(seed), 11)
    states = scatter_about(splits[0], (LAYERS, TOKENS, D), 1.0, 6.0, ((0, 8), (1, 4), (2, 8)))
    final_state = scatter_about(splits[1], (TOKENS, D), 1.0, 6.0, ((0, 4), (1, 8)))
    retained = draw_retained(jax.random.fold_in(splits[10], 71), 0)
    block_slot = jax.random.permutation(splits[3], BLOCKS).astype(jnp.int32)
    w_in = scatter_about(splits[4], (BLOCKS, D, DI), D ** -0.5, 0.0625, ((0, 8), (1, 8), (2, 4)))
    w_side = scatter_about(splits[5], (BLOCKS, D, 2 * NS + HEADS), (8 * D) ** -0.5, 0.0234375, ((0, 8), (1, 8)))
    w_out = scatter_about(splits[6], (BLOCKS, DI, D), DI ** -0.5, 0.09375, ((0, 8), (1, 4), (2, 8)))
    a_rate = jnp.clip(jnp.exp(math.log(0.5) - 4.6051702 * jax.random.uniform(splits[7], (BLOCKS, HEADS), jnp.float32) ** steps_of(splits[7], (BLOCKS, HEADS), ((0, 8),), -0.2, 0.2)), 0.005, 0.5)
    dt_bias = jnp.clip(jax.random.uniform(splits[8], (BLOCKS, HEADS), jnp.float32, -1.0, 1.0) * steps_of(splits[8], (BLOCKS, HEADS), ((0, 8),), -0.4, 0.0), -1.0, 1.0)
    skip = jnp.clip(jax.random.uniform(splits[9], (BLOCKS, HEADS), jnp.float32, -1.0, 1.0) * steps_of(splits[9], (BLOCKS, HEADS), ((0, 8),), -0.4, 0.0), -1.0, 1.0)
    return dict(states=states, final_state=final_state, retained=retained, block_slot=block_slot, w_in=w_in, w_side=w_side, w_out=w_out, a_rate=a_rate, dt_bias=dt_bias, skip=skip)


def mixer(values_in, writer, reader, step_raw, biases, rates, skips, seq_count):
    head_count, head_size, token_count = values_in.shape
    seq_len = token_count // seq_count
    step_size = jax.nn.softplus(step_raw + biases[None, :])
    log_decay = -(step_size * rates[None, :])
    log_decay = log_decay.reshape(seq_count, seq_len, head_count).transpose(0, 2, 1)
    cumulative = jnp.cumsum(log_decay, axis=2)
    differences = cumulative[:, :, :, None] - cumulative[:, :, None, :]
    causal = jnp.arange(seq_len)[:, None] >= jnp.arange(seq_len)[None, :]
    decays = jnp.where(causal, jnp.exp(jnp.where(causal, differences, 0.0)), 0.0)
    scores = jnp.einsum('stn,sun->stu', reader.reshape(seq_count, seq_len, -1), writer.reshape(seq_count, seq_len, -1), precision=lax.Precision.HIGHEST)
    weights = decays * scores[:, None]
    values_four = values_in.reshape(head_count, head_size, seq_count, seq_len)
    steps_in = values_four * step_size.reshape(seq_count, seq_len, head_count).transpose(2, 0, 1)[:, None]
    mixed_out = jnp.einsum('shtu,hpsu->hpst', weights, steps_in, precision=lax.Precision.HIGHEST)
    mixed_out = mixed_out + skips[:, None, None, None] * values_four
    return mixed_out.reshape(head_count, head_size, token_count)

def reference(states, final_state, retained, block_slot, w_in, w_side, w_out, a_rate, dt_bias, skip):
    layer_total = states.shape[0]
    block_rows = jnp.arange(BLOCKS, dtype=jnp.int32)
    owner_hit = block_slot[None, :] == block_rows[:, None]
    wanted = lax.optimization_barrier(jnp.sum(jnp.where(owner_hit, retained[None, :], 0), axis=1)).astype(jnp.int32)

    def one_block(items):
        layer, weight_in, weight_side, weight_out, rates, biases, skips = items
        source = lax.dynamic_index_in_dim(states, layer, 0, keepdims=False)
        following_index = jnp.minimum(layer + 1, layer_total - 1).astype(jnp.int32)
        following = lax.dynamic_index_in_dim(states, following_index, 0, keepdims=False)
        target = jnp.where(layer + 1 < layer_total, following, final_state)
        projected = jnp.dot(source, weight_in, preferred_element_type=jnp.float32)
        heads_first = projected.reshape(TOKENS, HEADS, P_SIZE).transpose(1, 2, 0)
        side = jnp.dot(source, weight_side, preferred_element_type=jnp.float32)

        def run(values_in, writer, reader, step_raw):
            return mixer(values_in, writer, reader, step_raw, biases, rates, skips, N_DP)
        mixed_out, pullback = jax.vjp(run, heads_first, side[:, :NS], side[:, NS:2 * NS], side[:, 2 * NS:])
        mixed_b = mixed_out.astype(jnp.bfloat16).reshape(DI, TOKENS)
        output = lax.dot_general(mixed_b, weight_out, (((0,), (0,)), ((), ())), preferred_element_type=jnp.float32)
        error = output - target.astype(jnp.float32)
        block_loss = jnp.mean(error * error)
        out_grad = (2.0 * error / TOKENS).astype(jnp.bfloat16)
        grad_out = jnp.dot(mixed_b, out_grad, preferred_element_type=jnp.float32).astype(jnp.bfloat16)
        mixed_grad = lax.dot_general(weight_out, out_grad, (((1,), (1,)), ((), ())), preferred_element_type=jnp.float32)
        grad_values, grad_writer, grad_reader, grad_steps = pullback(mixed_grad.reshape(HEADS, P_SIZE, TOKENS))
        side_grad = jnp.concatenate([grad_writer, grad_reader, grad_steps], axis=1).astype(jnp.bfloat16)
        grad_side = lax.dot_general(source, side_grad, (((0,), (0,)), ((), ())), preferred_element_type=jnp.float32).astype(jnp.bfloat16)
        values_grad = grad_values.astype(jnp.bfloat16).reshape(DI, TOKENS)
        grad_in = lax.dot_general(source, values_grad, (((0,), (1,)), ((), ())), preferred_element_type=jnp.float32).astype(jnp.bfloat16)
        return (grad_in, grad_side, grad_out, block_loss)
    grad_in, grad_side, grad_out, mean_loss = lax.map(one_block, (wanted, w_in, w_side, w_out, a_rate, dt_bias, skip))
    return (grad_in, grad_side, grad_out, mean_loss)
```

```python
import functools
from types import SimpleNamespace

import jax
import jax.numpy as jnp
from jax import lax
from jax.experimental import pallas as pl
from jax.experimental.pallas import tpu as pltpu
from jax.sharding import PartitionSpec as P

P_SIZE = 64
NS = 64
NZ = 2
MESH = pl.DeviceIdType.MESH
F32 = jnp.float32
BF = jnp.bfloat16
HI = lax.Precision.HIGHEST


def dot(a, b, ca=1, cb=0, precision=None):
    return lax.dot_general(
        a, b, (((ca,), (cb,)), ((), ())), preferred_element_type=F32, precision=precision
    )


def arrival(n):
    return sorted(range(1, n), key=lambda k: min(k, n - k))


def kernel(cfg, stop, states, final, retained, slot, w_in, w_side, w_out, a_rate, dt_bias, skip,
           g_in, g_side, g_out, loss, *scratch):
    b = SimpleNamespace(**dict(zip(cfg.names, scratch)))
    ND, SEC, NY = cfg.nd, cfg.sec, cfg.ny
    T, F, C, H = cfg.t, cfg.f, cfg.c, cfg.c // NZ
    HB, HH = cfg.hb, cfg.hb // NZ
    RC = T // SEC
    SIDE = T + HB
    d, s, t = lax.axis_index("dp"), lax.axis_index("section"), lax.axis_index("tensor")
    zh, y = t // NY, t % NY
    oz = 1 - zh

    def xdev(i):
        return (i, s, t)

    def ydev(i):
        return (d, s, zh * NY + i)

    def sdev(i):
        return (d, i, t)

    zdev = (d, s, oz * NY + y)

    bar = pltpu.get_barrier_semaphore()
    partners = (
        [xdev((d + k) % ND) for k in range(1, ND)]
        + [ydev((y + k) % NY) for k in range(1, NY)]
        + [sdev((s + k) % SEC) for k in range(1, SEC)]
        + [zdev]
    )
    for p in partners:
        pl.semaphore_signal(bar, inc=1, device_id=p, device_id_type=MESH)

    loads = [
        pltpu.make_async_copy(src, dst, b.load_sem.at[i])
        for i, (src, dst) in enumerate((
            (states.at[:, pl.ds(pl.multiple_of(s * RC, 16), RC)], b.layers.at[pl.ds(2 * s, 2)]),
            (w_side.at[0], b.wside), (w_in.at[0], b.win), (w_out.at[0], b.wout), (final, b.final),
        ))
    ]
    for cp in loads:
        cp.start()
    pl.semaphore_wait(bar, len(partners))

    def send(src, dst, sems, i, dev):
        cp = pltpu.make_async_remote_copy(
            src_ref=src, dst_ref=dst, send_sem=sems.at[0, i], recv_sem=sems.at[1, i],
            device_id=dev, device_id_type=MESH,
        )
        return cp

    def rows(i, n=None):
        n = T if n is None else n
        return pl.ds(pl.multiple_of(i * n, 16), n)

    def half(i):
        return pl.ds(pl.multiple_of(i * H, 128), H)

    pending = []

    def go(cp):
        cp.start()
        pending.append(cp)
        return cp

    hop1 = [
        go(send(states.at[:, rows((s + k) % SEC, RC)], b.layers.at[pl.ds(2 * s, 2)], b.h1_sem, k, sdev((s + k) % SEC)))
        for k in range(1, SEC)
    ]
    wanted = []
    for i in range(SEC):
        layer = jnp.int32(0)
        for r in range(SEC):
            layer = layer + jnp.where(slot[r] == i, retained[r], 0)
        wanted.append(layer)
    mine = jnp.int32(0)
    for i in range(SEC):
        mine = mine + jnp.where(s == i, wanted[i], 0)

    def wanted_of(i):
        out = jnp.int32(0)
        for j in range(SEC):
            out = out + jnp.where(i == j, wanted[j], 0)
        return out

    loads[0].wait()
    loads[1].wait()
    heads_all = cfg.heads
    pick = (
        lax.broadcasted_iota(jnp.int32, (HB, heads_all), 1)
        == lax.broadcasted_iota(jnp.int32, (HB, heads_all), 0) + d * HB
    )
    b.wstep[...] = dot(pick.astype(BF), b.wside[:, 2 * NS:], 1, 1).astype(BF)

    for cp in hop1:
        cp.wait_recv()
    hop2 = []
    for k in range(1, SEC):
        to = (s + k) % SEC
        b.stage.at[0, k][...] = b.layers[wanted_of(to)]
        hop2.append(go(send(b.stage.at[0, k], b.src.at[rows(d), :].at[rows(s, RC)], b.h2_sem, k, sdev(to))))
    b.src.at[rows(d), :].at[rows(s, RC)][...] = b.layers[mine]
    hop3 = []
    for k in range(1, SEC):
        to = (s + k) % SEC
        b.stage.at[1, k][...] = b.layers[jnp.minimum(wanted_of(to) + 1, 2 * SEC - 1)]
        hop3.append(go(send(b.stage.at[1, k], b.tgt.at[rows(s, RC)], b.h3_sem, k, sdev(to))))
    b.tgt.at[rows(s, RC)][...] = b.layers[jnp.minimum(mine + 1, 2 * SEC - 1)]
    for cp in hop2:
        cp.wait_recv()

    gather = {
        k: go(send(b.src.at[rows(d)], b.src.at[rows(d)], b.ag_sem, k, xdev((d + k) % ND)))
        for k in arrival(ND)
    }
    loads[2].wait()

    NB = 256

    def product(q, lhs, w, out, rel, transposed=False):
        def step(n, carry):
            cols = pl.ds(pl.multiple_of(n * NB, NB), NB)
            w_n = w[cols, :] if transposed else w[:, cols]
            out.at[rel][:, cols] = dot(lhs[rows(q), :], w_n, 1, 1 if transposed else 0).astype(BF)
            return carry

        lax.fori_loop(0, out.shape[2] // NB, step, 0)

    def c_copies(rel):
        to = ydev((y + rel) % NY)
        return (
            send(b.psend.at[rel], b.prec.at[rel], b.c_sem, rel, to),
            send(b.ssend.at[rel], b.srec.at[rel], b.cs_sem, rel, to),
        )

    for k in [0] + arrival(ND):
        if k:
            gather[k].wait_recv()
        q = (d - k) % ND
        rel = (q - y) % NY
        product(q, b.src, b.win, b.psend, rel)
        b.ssend.at[rel][:T, :] = dot(b.src[rows(q), :], b.wside[:, : 2 * NS]).astype(BF)
        b.ssend.at[rel][T:, :] = dot(b.wstep[...], b.src[rows(q), :], 1, 1).astype(BF)

        @pl.when(rel != 0)
        def _():
            for cp in c_copies(rel):
                cp.start()

    for q in range(ND):
        for j in range(F // 128):
            b.srct[128 * j: 128 * (j + 1), T * q: T * (q + 1)] = (
                b.src[T * q: T * (q + 1), 128 * j: 128 * (j + 1)].T
            )
    for rel in range(1, NY):
        for cp in c_copies(rel):
            cp.wait_recv()
    part = b.psend.at[0][:, half(oz)].astype(F32)
    for rel in range(1, NY):
        part = part + b.prec.at[rel][:, half(oz)].astype(F32)
    b.zsend[...] = part.astype(BF)
    cz = go(send(b.zsend, b.zrec, b.z_sem, 0, zdev))
    part = b.ssend[0].astype(F32)
    for rel in range(1, NY):
        part = part + b.srec[rel].astype(F32)
    b.zssend[...] = part.astype(BF)
    czs = go(send(b.zssend, b.zsrec, b.z_sem, 1, zdev))
    b.side[...] = part
    part = b.psend.at[0][:, half(zh)].astype(F32)
    for rel in range(1, NY):
        part = part + b.prec.at[rel][:, half(zh)].astype(F32)
    cz.wait_recv()
    b.vals[...] = part + b.zrec[...].astype(F32)
    czs.wait_recv()
    b.side[...] += b.zsrec[...].astype(F32)

    head0 = d * HB + zh * HH

    def column(ref):
        at = lax.broadcasted_iota(jnp.int32, (HH, 1), 0)
        out = jnp.zeros((HH, 1), F32)
        for k in range(HH):
            out = jnp.where(at == k, ref[0, head0 + k], out)
        return out

    rate, bias = column(a_rate), column(dt_bias)
    r_t = lax.broadcasted_iota(jnp.int32, (T, T), 0)
    r_u = lax.broadcasted_iota(jnp.int32, (T, T), 1)
    causal = r_t >= r_u
    low = r_u < NS
    raw = b.side[pl.ds(pl.multiple_of(T + zh * HH, 8), HH), :] + bias
    step = jax.nn.softplus(raw)
    cum = dot(-(step * rate), (r_t <= r_u).astype(F32), precision=HI)
    rw = b.side[:T, :]
    wr = pltpu.roll(rw, NS, 1)
    scores = dot(jnp.where(low, wr, 0.0), rw, 1, 1, precision=HI)
    cum_cols = jnp.concatenate([cum] * (T // HH), axis=0).T
    for k in range(HH):
        diff = cum_cols[:, k: k + 1] - cum[k: k + 1, :]
        b.decay[k] = jnp.where(causal, jnp.exp(jnp.where(causal, diff, 0.0)), 0.0)
    for j in range(H // 128):
        cols = slice(128 * j, 128 * (j + 1))
        v = b.vals[:, cols]
        vb = v.astype(BF)
        outs = []
        for k in (2 * j, 2 * j + 1):
            w = (b.decay[k] * scores * step[k: k + 1, :]).astype(BF)
            outs.append(dot(w, vb))
        y2 = jnp.where(low, outs[0], outs[1])
        b.pure[:, cols] = y2
        skips = jnp.where(low, skip[0, head0 + 2 * j], skip[0, head0 + 2 * j + 1])
        b.mhalf[:, cols] = (y2 + skips * v).astype(BF)
    b.mix.at[rows(y)][:, half(zh)] = b.mhalf[...]

    def gather_z(buf, sems):
        return send(b.mhalf if buf is b.mix else b.vghalf, buf.at[rows(y), half(zh)], sems, 0, zdev)

    def gather_y(buf, sems, rel):
        return send(
            b.mhalf if buf is b.mix else b.vghalf, buf.at[rows(y), half(zh)], sems, rel, ydev((y + rel) % NY)
        )

    def forward_y(buf, sems, rel):
        return send(
            buf.at[rows(y), half(oz)], buf.at[rows(y), half(oz)], sems, NY + rel, ydev((y + rel) % NY)
        )

    go(gather_z(b.mix, b.e_sem))
    for rel in arrival(NY):
        go(gather_y(b.mix, b.e_sem, rel))
    gather_z(b.mix, b.e_sem).wait_recv()
    for rel in arrival(NY):
        go(forward_y(b.mix, b.e_sem, rel))
    loads[3].wait()

    def f_copy(rel):
        return send(b.osend.at[rel], b.orec.at[rel], b.f_sem, rel, xdev((d + rel) % ND))

    for k in [0] + arrival(NY):
        if k:
            gather_y(b.mix, b.e_sem, k).wait_recv()
            forward_y(b.mix, b.e_sem, k).wait_recv()
        q = (y - k) % NY
        rel = (q - d) % ND
        product(q, b.mix, b.wout, b.osend, rel)

        @pl.when(rel != 0)
        def _():
            f_copy(rel).start()

    for q in range(NY):
        for j in range(C // 128):
            b.mixt[128 * j: 128 * (j + 1), T * q: T * (q + 1)] = (
                b.mix[T * q: T * (q + 1), 128 * j: 128 * (j + 1)].T
            )
    loads[4].wait()
    for cp in hop3:
        cp.wait_recv()
    inner = mine + 1 < 2 * SEC
    for rel in range(1, ND):
        f_copy(rel).wait_recv()
    total = jnp.zeros((8, 128), F32)
    for j in range(F // 128):
        cols = slice(128 * j, 128 * (j + 1))
        out = b.osend[0, :, cols].astype(F32)
        for rel in range(1, ND):
            out = out + b.orec[rel, :, cols].astype(F32)
        goal = jnp.where(inner, b.tgt[:, cols].astype(F32), b.final[:, cols].astype(F32))
        err = out - goal
        b.ogown[:, cols] = (2.0 * err / (T * ND)).astype(BF)
        total = total + jnp.sum((err * err).reshape(T // 8, 8, 128), axis=0)
    b.og.at[rows(d)][...] = b.ogown[...]
    b.lsum[0] = total

    def h_copy(k):
        return send(b.ogown, b.og.at[rows(d)], b.h_sem, k, xdev((d + k) % ND))

    for k in arrival(ND):
        go(h_copy(k))

    def loss_x(k):
        return send(b.lsum.at[0], b.lrec.at[k], b.l_sem, k, xdev((d + k) % ND))

    def loss_y(k):
        return send(b.lsum.at[1], b.lrec.at[ND + k], b.l_sem, ND + k, ydev((y + k) % NY))

    def loss_z():
        return send(b.lsum.at[2], b.lrec.at[ND + NY], b.l_sem, ND + NY, zdev)

    for k in range(1, ND):
        go(loss_x(k))

    def i_copy(rel):
        return send(b.isend.at[rel], b.irec.at[rel], b.i_sem, rel, ydev((y + rel) % NY))

    for k in [0] + arrival(ND):
        if k:
            h_copy(k).wait_recv()
        q = (d - k) % ND
        rel = (q - y) % NY
        product(q, b.og, b.wout, b.isend, rel, transposed=True)

        @pl.when(rel != 0)
        def _():
            i_copy(rel).start()

    total = b.lsum[0]
    for k in range(1, ND):
        loss_x(k).wait_recv()
        total = total + b.lrec[k]
    b.lsum[1] = total
    for k in range(1, NY):
        go(loss_y(k))
    for rel in range(1, NY):
        i_copy(rel).wait_recv()
    part = b.isend.at[0][:, half(oz)].astype(F32)
    for rel in range(1, NY):
        part = part + b.irec.at[rel][:, half(oz)].astype(F32)
    b.izsend[...] = part.astype(BF)
    iz = go(send(b.izsend, b.izrec, b.z_sem, 2, zdev))

    def store(n, carry):
        at = pl.ds(pl.multiple_of(n * 256, 256), 256)
        b.gout[at, :] = dot(b.mixt[at, :], b.og[...]).astype(BF)
        return carry

    lax.fori_loop(0, C // 256, store, 0)
    out_copy = pltpu.make_async_copy(b.gout, g_out.at[0], b.store_sem.at[0])
    out_copy.start()
    total = b.lsum[1]
    for k in range(1, NY):
        loss_y(k).wait_recv()
        total = total + b.lrec[ND + k]
    b.lsum[2] = total
    go(loss_z())
    iz.wait_recv()

    dscore = jnp.zeros((T, T), F32)
    sums, rowsums = [], []
    at_lane = lax.broadcasted_iota(jnp.int32, (T, 128), 1)
    rowcols = jnp.zeros((T, 128), F32)
    for j in range(H // 128):
        cols = slice(128 * j, 128 * (j + 1))
        own = pl.ds(pl.multiple_of(zh * H + 128 * j, 128), 128)
        g = b.isend.at[0][:, own].astype(F32)
        for rel in range(1, NY):
            g = g + b.irec.at[rel][:, own].astype(F32)
        g = g + b.izrec[:, cols].astype(F32)
        gb = g.astype(BF)
        v = b.vals[:, cols]
        prod = g * b.pure[:, cols]
        outs = []
        for e in (0, 1):
            k = 2 * j + e
            here = low if e == 0 else jnp.logical_not(low)
            x = dot(gb, jnp.where(here, v, 0.0).astype(BF), 1, 1)
            decay = b.decay[k]
            st = step[k: k + 1, :]
            xd = x * decay
            dscore = dscore + xd * st
            sums.append(jnp.sum(xd * scores, axis=0, keepdims=True))
            rowcols = jnp.where(
                at_lane == k, jnp.sum(jnp.where(here, prod, 0.0), axis=1, keepdims=True), rowcols
            )
            wt = (decay * scores * st).T.astype(BF)
            outs.append(dot(wt, gb))
        skips = jnp.where(low, skip[0, head0 + 2 * j], skip[0, head0 + 2 * j + 1])
        b.vghalf[:, cols] = (jnp.where(low, outs[0], outs[1]) + skips * g).astype(BF)
    b.vg.at[rows(y)][:, half(zh)] = b.vghalf[...]
    go(gather_z(b.vg, b.k_sem))
    for rel in arrival(NY):
        go(gather_y(b.vg, b.k_sem, rel))
    dstep = jnp.concatenate(sums, axis=0)
    dcum = rowcols.T[:HH, :] - step * dstep
    ddecay = dot(dcum, causal.astype(F32), precision=HI)
    draw = (dstep - rate * ddecay) * jax.nn.sigmoid(raw)
    drw = jnp.where(low, dot(dscore.T, wr, precision=HI), dot(dscore, wr, precision=HI))
    in_half = lax.broadcasted_iota(jnp.int32, (HB, T), 0) // HH == zh
    dsteps = jnp.where(in_half, jnp.concatenate([draw] * NZ, axis=0), 0.0)

    b.j1send[:T, :] = drw.astype(BF)
    b.j1send[T:, :] = dsteps.astype(BF)
    j1 = go(send(b.j1send, b.j1rec, b.z_sem, 3, zdev))
    j1.wait_recv()
    b.j2send[:T, :] = (drw + b.j1rec[:T, :].astype(F32)).astype(BF)
    b.j2send[T:, :] = (dsteps + b.j1rec[T:, :].astype(F32)).astype(BF)
    b.j2rec.at[d][...] = b.j2send[...]

    def j2_copy(k):
        return send(b.j2send, b.j2rec.at[d], b.j2_sem, k, xdev((d + k) % ND))

    for k in arrival(ND):
        go(j2_copy(k))
    gather_z(b.vg, b.k_sem).wait_recv()
    for rel in arrival(NY):
        go(forward_y(b.vg, b.k_sem, rel))
    for k in arrival(ND):
        j2_copy(k).wait_recv()
    part = b.j2rec[0, :T, :].astype(F32)
    for q in range(1, ND):
        part = part + b.j2rec[q, :T, :].astype(F32)
    b.j3send[:T, :] = part.astype(BF)
    for q in range(ND):
        b.j3send[T + HB * q: T + HB * (q + 1), :] = b.j2rec[q, T:, :]
    b.j3rec.at[y][...] = b.j3send[...]

    def j3_copy(k):
        return send(b.j3send, b.j3rec.at[y], b.j3_sem, k, ydev((y + k) % NY))

    for k in arrival(NY):
        go(j3_copy(k))
    loss_z().wait_recv()
    b.lout[...] = (
        jnp.zeros((8, 128), F32) + jnp.sum(b.lsum[2] + b.lrec[ND + NY]) / (T * ND * F * NY * NZ)
    )
    loss_copy = pltpu.make_async_copy(b.lout, loss, b.store_sem.at[1])
    loss_copy.start()

    for k in arrival(NY):
        gather_y(b.vg, b.k_sem, k).wait_recv()
        forward_y(b.vg, b.k_sem, k).wait_recv()
    in_copies = []
    for n in range(F // 128 // 2 if F >= 256 else 1):
        w = min(256, F)
        b.gin[w * n: w * (n + 1), :] = dot(b.srct[w * n: w * (n + 1), :], b.vg[...]).astype(BF)
        cp = pltpu.make_async_copy(
            b.gin.at[pl.ds(w * n, w)], g_in.at[0, pl.ds(w * n, w)], b.store_sem.at[2 + n]
        )
        cp.start()
        in_copies.append(cp)
    for k in arrival(NY):
        j3_copy(k).wait_recv()
    for q in range(NY):
        b.sg[T * q: T * (q + 1), : 2 * NS] = b.j3rec[q, :T, :]
        b.sg[T * q: T * (q + 1), 2 * NS:] = b.j3rec[q, T:, :].T
    b.gside[...] = dot(b.srct[...], b.sg[...]).astype(BF)
    side_copy = pltpu.make_async_copy(b.gside, g_side.at[0], b.store_sem.at[1 + 1 + cfg.nin])
    side_copy.start()

    for cp in pending:
        cp.wait_send()
    for rel in range(1, NY):
        for cp in c_copies(rel):
            cp.wait_send()
        i_copy(rel).wait_send()
    for rel in range(1, ND):
        f_copy(rel).wait_send()
    out_copy.wait()
    loss_copy.wait()
    side_copy.wait()
    for cp in in_copies:
        cp.wait()


def local(states, final_state, retained, block_slot, w_in, w_side, w_out, a_rate, dt_bias, skip):
    nd, sec, nt = lax.axis_size("dp"), lax.axis_size("section"), lax.axis_size("tensor")
    ny = nt // NZ
    t, f = final_state.shape
    c = w_in.shape[2]
    heads = a_rate.shape[1]
    hb = c // P_SIZE
    side = t + hb
    sd = 2 * NS + heads
    h = c // NZ
    n = t * nd
    nin = max(1, f // 256)
    assert ny == nd and t == 128
    V = pltpu.VMEM

    def sems(k):
        return pltpu.SemaphoreType.DMA((2, k))

    scratch = dict(
        layers=V((2 * sec, t // sec, f), BF), stage=V((2, sec, t // sec, f), BF),
        src=V((n, f), BF), tgt=V((t, f), BF), final=V((t, f), BF), srct=V((f, n), BF),
        win=V((f, c), BF), wside=V((f, sd), BF), wout=V((c, f), BF), wstep=V((hb, f), BF),
        psend=V((ny, t, c), BF), prec=V((ny, t, c), BF),
        ssend=V((ny, side, 128), BF), srec=V((ny, side, 128), BF),
        zsend=V((t, h), BF), zrec=V((t, h), BF), zssend=V((side, 128), BF), zsrec=V((side, 128), BF),
        side=V((side, 128), F32), vals=V((t, h), F32), pure=V((t, h), F32),
        decay=V((hb // NZ, t, t), F32), mhalf=V((t, h), BF), mix=V((n, c), BF), mixt=V((c, n), BF),
        osend=V((nd, t, f), BF), orec=V((nd, t, f), BF), ogown=V((t, f), BF), og=V((n, f), BF),
        lsum=V((3, 8, 128), F32), lrec=V((nd + ny + 1, 8, 128), F32), lout=V((8, 128), F32),
        isend=V((ny, t, c), BF), irec=V((ny, t, c), BF), izsend=V((t, h), BF), izrec=V((t, h), BF),
        gout=V((c, f), BF), vghalf=V((t, h), BF), vg=V((n, c), BF),
        j1send=V((side, 128), BF), j1rec=V((side, 128), BF),
        j2send=V((side, 128), BF), j2rec=V((nd, side, 128), BF),
        j3send=V((t + heads, 128), BF), j3rec=V((ny, t + heads, 128), BF), sg=V((n, sd), BF),
        gin=V((f, c), BF), gside=V((f, sd), BF),
        load_sem=pltpu.SemaphoreType.DMA((5,)), store_sem=pltpu.SemaphoreType.DMA((3 + nin,)),
        h1_sem=sems(sec), h2_sem=sems(sec), h3_sem=sems(sec), ag_sem=sems(nd),
        c_sem=sems(ny), cs_sem=sems(ny), z_sem=sems(4), e_sem=sems(2 * ny), f_sem=sems(nd),
        h_sem=sems(nd), i_sem=sems(ny), l_sem=sems(nd + ny + 1), k_sem=sems(2 * ny),
        j2_sem=sems(nd), j3_sem=sems(ny),
    )
    cfg = SimpleNamespace(
        names=tuple(scratch), nd=nd, sec=sec, ny=ny, t=t, f=f, c=c, hb=hb, heads=heads, nin=nin
    )
    hbm = pl.BlockSpec(memory_space=pl.ANY)
    smem = pl.BlockSpec(memory_space=pltpu.SMEM)
    g_in, g_side, g_out, loss = pl.pallas_call(
        functools.partial(kernel, cfg, None),
        out_shape=(
            jax.ShapeDtypeStruct(w_in.shape, BF), jax.ShapeDtypeStruct(w_side.shape, BF),
            jax.ShapeDtypeStruct(w_out.shape, BF), jax.ShapeDtypeStruct((8, 128), F32),
        ),
        in_specs=[hbm, hbm, smem, smem, hbm, hbm, hbm, smem, smem, smem],
        out_specs=(hbm, hbm, hbm, hbm),
        scratch_shapes=list(scratch.values()),
        compiler_params=pltpu.CompilerParams(
            collective_id=0, has_side_effects=True, vmem_limit_bytes=48 << 20
        ),
        name="distill",
    )(states, final_state, retained, block_slot, w_in, w_side, w_out, a_rate, dt_bias, skip)
    return g_in, g_side, g_out, loss[0, :1]


def solution(mesh):
    placed = (
        P("section", "dp", "tensor"),
        P("dp", "tensor"),
        P(),
        P(),
        P("section", "tensor", "dp"),
        P("section", "tensor", None),
        P("section", "dp", "tensor"),
        P("section", None),
        P("section", None),
        P("section", None),
    )
    return jax.shard_map(
        local,
        mesh=mesh,
        in_specs=placed,
        out_specs=(
            P("section", "tensor", "dp"),
            P("section", "tensor", None),
            P("section", "dp", "tensor"),
            P("section"),
        ),
        check_vma=False,
    )
```

```python
import functools
from types import SimpleNamespace

import jax
import jax.numpy as jnp
from jax import lax
from jax.experimental import pallas as pl
from jax.experimental.pallas import tpu as pltpu
from jax.sharding import PartitionSpec as P

P_SIZE = 64
NS = 64
NZ = 2
MESH = pl.DeviceIdType.MESH
F32 = jnp.float32
BF = jnp.bfloat16
HI = lax.Precision.HIGHEST


def dot(a, b, ca=1, cb=0, precision=None):
    return lax.dot_general(
        a, b, (((ca,), (cb,)), ((), ())), preferred_element_type=F32, precision=precision
    )


class Copy:
    def __init__(self, copy, key, due):
        self.copy, self.key, self.due = copy, key, due
        self.start, self.wait_send = copy.start, copy.wait_send

    def wait_recv(self):
        self.copy.wait_recv()
        self.due.pop(self.key, None)


def arrival(n):
    return sorted(range(1, n), key=lambda k: min(k, n - k))


def kernel(cfg, stop, states, final, retained, slot, w_in, w_side, w_out, a_rate, dt_bias, skip,
           g_in, g_side, g_out, loss, *scratch):
    b = SimpleNamespace(**dict(zip(cfg.names, scratch)))
    ND, SEC, NY = cfg.nd, cfg.sec, cfg.ny
    T, F, C, H = cfg.t, cfg.f, cfg.c, cfg.c // NZ
    HB, HH = cfg.hb, cfg.hb // NZ
    NC = SEC // 2
    RC, CR = T // SEC, T // NC
    W = 2 * NS
    d, s, t = lax.axis_index("dp"), lax.axis_index("section"), lax.axis_index("tensor")
    zh, y = t // NY, t % NY
    oz = 1 - zh
    zl, core = s // 2, s % 2

    def xdev(i):
        return (i, s, t)

    def ydev(i):
        return (d, s, zh * NY + i)

    zdev = (d, s, oz * NY + y)

    if NC == 4:
        chips = [zl, zl + 1 - 2 * (zl % 2), (zl + 2) % 4, 3 - zl]
    else:
        chips = [zl, 1 - zl]
    sections = [2 * c + k for c in chips for k in (core, 1 - core)]
    far_first = [m for i in (2, 3, 1, 0) for m in (2 * i, 2 * i + 1) if 0 < m < SEC]

    def sdev(m):
        return (d, sections[m], t)

    bar = pltpu.get_barrier_semaphore()
    partners = (
        [sdev(m) for m in far_first]
        + [xdev((d + k) % ND) for k in range(1, ND)]
        + [ydev((y + k) % NY) for k in range(1, NY)]
        + [zdev]
    )
    for p in partners:
        pl.semaphore_signal(bar, inc=1, device_id=p, device_id_type=MESH)

    def rows(i, n):
        return pl.ds(pl.multiple_of(i * n, 16), n)

    def half(i):
        return pl.ds(pl.multiple_of(i * H, 128), H)

    loads = [
        pltpu.make_async_copy(src, dst, b.load_sem.at[i])
        for i, (src, dst) in enumerate((
            (states.at[:, rows(s, RC)], b.layers.at[pl.ds(2 * s, 2)]),
            (retained, b.retained), (slot, b.slot), (w_side.at[0], b.wside), (w_in.at[0], b.win),
            (a_rate, b.rate), (dt_bias, b.bias), (skip, b.skip), (w_out.at[0], b.wout), (final, b.final),
        ))
    ]
    for cp in loads:
        cp.start()
    loading = dict(enumerate(loads))

    def loaded(*which):
        for i in which:
            loading.pop(i).wait()

    def send(src, dst, sems, i, dev):
        cp = pltpu.make_async_remote_copy(
            src_ref=src, dst_ref=dst, send_sem=sems.at[0, i], recv_sem=sems.at[1, i],
            device_id=dev, device_id_type=MESH,
        )
        return Copy(cp, (id(sems), i), due)

    pending, due = [], {}

    def go(cp):
        cp.start()
        pending.append(cp)
        due[cp.key] = cp
        return cp

    def finish():
        for cp in list(due.values()):
            cp.wait_recv()
        for i in list(loading):
            loaded(i)
        for cp in pending:
            cp.wait_send()

    pl.semaphore_wait(bar, len(partners))

    hop1 = [
        go(send(states.at[:, rows(sections[m], RC)], b.layers.at[pl.ds(2 * s, 2)], b.h1_sem, m, sdev(m)))
        for m in far_first
    ]
    loaded(0, 1, 2, 3)
    wanted = []
    for i in range(SEC):
        layer = jnp.int32(0)
        for r in range(SEC):
            layer = layer + jnp.where(b.slot[r] == i, b.retained[r], 0)
        wanted.append(layer)

    def wanted_of(i):
        out = jnp.int32(0)
        for j in range(SEC):
            out = out + jnp.where(i == j, wanted[j], 0)
        return out

    layer_of = [wanted_of(i) for i in sections]
    pick = (
        lax.broadcasted_iota(jnp.int32, (HB, cfg.heads), 1)
        == lax.broadcasted_iota(jnp.int32, (HB, cfg.heads), 0) + d * HB
    )
    b.wstep[...] = dot(pick.astype(BF), b.wside[W:, :]).astype(BF)

    for cp in hop1:
        cp.wait_recv()
    mine = rows(core, RC)
    b.src[zl, d, mine, :] = b.layers[layer_of[0]]
    hop2 = {}
    for m in range(1, SEC):
        b.stage[0, m] = b.layers[layer_of[m]]
        hop2[m] = go(send(b.stage.at[0, m], b.src.at[zl, d, mine], b.h2_sem, m, sdev(m)))

    def g_copy(i, k):
        at = b.src.at[chips[i], d]
        return send(at, at, b.g_sem, i * ND + k, xdev((d + k) % ND))

    for i in range(NC):
        for m in (2 * i, 2 * i + 1):
            if m:
                hop2[m].wait_recv()
        for k in arrival(ND):
            go(g_copy(i, k))
    hop3 = []
    for m in range(1, SEC):
        b.stage[1, m] = b.layers[jnp.minimum(layer_of[m] + 1, 2 * SEC - 1)]
        hop3.append(go(send(b.stage.at[1, m], b.tgt.at[rows(s, RC)], b.h3_sem, m, sdev(m))))
    b.tgt[rows(s, RC), :] = b.layers[jnp.minimum(layer_of[0] + 1, 2 * SEC - 1)]
    loaded(4)

    NB = 256

    def product(lhs, c, w, out, i, transposed=False):
        def step(n, carry):
            cols = pl.ds(pl.multiple_of(n * NB, NB), NB)
            w_n = w[cols, :] if transposed else w[:, cols]
            x = lhs[c].reshape(ND * CR, lhs.shape[3])
            r = dot(x, w_n, 1, 1 if transposed else 0).astype(BF)
            out[i, :, :, cols] = r.reshape(ND, CR, NB)
            return carry

        lax.fori_loop(0, (w.shape[0] if transposed else w.shape[1]) // NB, step, 0)

    def c_copy(i, rel):
        q = (y + rel) % NY
        return send(b.psend.at[i, q], b.prec.at[i, rel], b.c_sem, i * NY + rel, ydev(q))

    def z_copy(i):
        return send(b.zsend.at[i], b.zrec.at[i], b.z_sem, i, zdev)

    def c_step(i):
        for k in arrival(ND):
            g_copy(i, k).wait_recv()
        c = chips[i]
        product(b.src, c, b.win, b.psend, i)
        x = b.src[c].reshape(ND * CR, F)
        b.psend[i, :, :, C:] = dot(x, b.wside[:W, :], 1, 1).astype(BF).reshape(ND, CR, W)
        for rel in arrival(NY):
            go(c_copy(i, rel))

    def c_sum(i):
        for rel in range(1, NY):
            c_copy(i, rel).wait_recv()

        def total(cols):
            out = b.psend[i, y, :, cols].astype(F32)
            for rel in range(1, NY):
                out = out + b.prec[i, rel, :, cols].astype(F32)
            return out

        b.zsend[i, :, :H] = total(half(oz)).astype(BF)
        side = total(slice(C, C + W))
        b.zsend[i, :, H:] = side.astype(BF)
        go(z_copy(i))
        here = rows(chips[i], CR)
        b.vals[here, :] = total(half(zh))
        b.rw[here, :] = side

    def st_copy(rel):
        return send(b.stsend.at[rel], b.strec.at[rel], b.st_sem, rel, ydev((y + rel) % NY))

    for i in range(NC):
        c_step(i)
        if i:
            c_sum(i - 1)
    for rel in arrival(NY) + [0]:
        x = b.src[:, (y + rel) % NY].reshape(T, F)
        b.stsend[rel] = dot(b.wstep[...], x, 1, 1).astype(BF)
        if rel:
            go(st_copy(rel))
    for c in range(NC):
        for j in range(F // 128):
            b.srct[128 * j: 128 * (j + 1), ND * CR * c: ND * CR * (c + 1)] = (
                b.src[c, :, :, 128 * j: 128 * (j + 1)].reshape(ND * CR, 128).T
            )
    c_sum(NC - 1)
    steps = b.stsend[0].astype(F32)
    for rel in range(1, NY):
        st_copy(rel).wait_recv()
        steps = steps + b.strec[rel].astype(F32)
    b.stz[0] = steps.astype(BF)
    stz = go(send(b.stz.at[0], b.stz.at[1], b.st_sem, NY, zdev))
    loaded(5, 6, 7)
    for i in range(NC):
        z_copy(i).wait_recv()
        here = rows(chips[i], CR)
        b.vals[here, :] += b.zrec[i, :, :H].astype(F32)
        b.rw[here, :] += b.zrec[i, :, H:].astype(F32)
    stz.wait_recv()
    b.steps[...] = steps + b.stz[1].astype(F32)

    head0 = d * HB + zh * HH

    def column(ref):
        at = lax.broadcasted_iota(jnp.int32, (HH, 1), 0)
        out = jnp.zeros((HH, 1), F32)
        for k in range(HH):
            out = jnp.where(at == k, ref[0, head0 + k], out)
        return out

    rate, bias = column(b.rate), column(b.bias)
    r_t = lax.broadcasted_iota(jnp.int32, (T, T), 0)
    r_u = lax.broadcasted_iota(jnp.int32, (T, T), 1)
    causal = r_t >= r_u
    low = r_u < NS
    raw = b.steps[pl.ds(pl.multiple_of(zh * HH, 8), HH), :] + bias
    step = jax.nn.softplus(raw)
    cum = dot(-(step * rate), (r_t <= r_u).astype(F32), precision=HI)
    rw = b.rw[...]
    wr = pltpu.roll(rw, NS, 1)
    scores = dot(jnp.where(low, wr, 0.0), rw, 1, 1, precision=HI)
    cum_cols = jnp.concatenate([cum] * (T // HH), axis=0).T
    for k in range(HH):
        diff = cum_cols[:, k: k + 1] - cum[k: k + 1, :]
        b.decay[k] = jnp.where(causal, jnp.exp(jnp.where(causal, diff, 0.0)), 0.0)

    def lanes(j):
        return pl.ds(pl.multiple_of(zh * H + 128 * j, 128), 128)

    for j in range(H // 128):
        cols = slice(128 * j, 128 * (j + 1))
        v = b.vals[:, cols]
        vb = v.astype(BF)
        outs = []
        for k in (2 * j, 2 * j + 1):
            w = (b.decay[k] * scores * step[k: k + 1, :]).astype(BF)
            outs.append(dot(w, vb))
        y2 = jnp.where(low, outs[0], outs[1])
        b.pure[:, cols] = y2
        skips = jnp.where(low, b.skip[0, head0 + 2 * j], b.skip[0, head0 + 2 * j + 1])
        b.mix[:, y, :, lanes(j)] = (y2 + skips * v).astype(BF).reshape(NC, CR, 128)

    def spread_z(buf, sems, c):
        at = buf.at[c, y, :, half(zh)]
        return send(at, at, sems, c, zdev)

    def spread_y(buf, sems, c, rel, which):
        at = buf.at[c, y, :, half(oz if which else zh)]
        return send(at, at, sems, NC + (2 * c + which) * NY + rel, ydev((y + rel) % NY))

    def spread(buf, sems):
        for c in range(NC):
            go(spread_z(buf, sems, c))
            for rel in arrival(NY):
                go(spread_y(buf, sems, c, rel, 0))

    def spread_on(buf, sems):
        for c in range(NC):
            spread_z(buf, sems, c).wait_recv()
            for rel in arrival(NY):
                go(spread_y(buf, sems, c, rel, 1))

    def spread_done(buf, sems, c):
        for rel in arrival(NY):
            for which in (0, 1):
                spread_y(buf, sems, c, rel, which).wait_recv()

    spread(b.mix, b.e_sem)
    loaded(8)
    spread_on(b.mix, b.e_sem)

    def f_copy(c, rel):
        q = (d + rel) % ND
        return send(b.osend.at[c, q], b.orec.at[c, rel], b.f_sem, c * ND + rel, xdev(q))

    for c in range(NC):
        spread_done(b.mix, b.e_sem, c)
        product(b.mix, c, b.wout, b.osend, c)
        for rel in arrival(ND):
            go(f_copy(c, rel))
    for c in range(NC):
        for j in range(C // 128):
            b.mixt[128 * j: 128 * (j + 1), NY * CR * c: NY * CR * (c + 1)] = (
                b.mix[c, :, :, 128 * j: 128 * (j + 1)].reshape(NY * CR, 128).T
            )
    loaded(9)
    for cp in hop3:
        cp.wait_recv()
    inner = layer_of[0] + 1 < 2 * SEC

    def h_copy(c, k):
        at = b.og.at[c, d]
        return send(at, at, b.h_sem, c * ND + k, xdev((d + k) % ND))

    total = jnp.zeros((8, 128), F32)
    for c in range(NC):
        for rel in range(1, ND):
            f_copy(c, rel).wait_recv()
        for j in range(F // 128):
            cols = slice(128 * j, 128 * (j + 1))
            here = slice(CR * c, CR * (c + 1))
            out = b.osend[c, d, :, cols].astype(F32)
            for rel in range(1, ND):
                out = out + b.orec[c, rel, :, cols].astype(F32)
            goal = jnp.where(inner, b.tgt[here, cols].astype(F32), b.final[here, cols].astype(F32))
            err = out - goal
            b.og[c, d, :, cols] = (2.0 * err / (T * ND)).astype(BF)
            total = total + jnp.sum((err * err).reshape(CR // 8, 8, 128), axis=0)
        for k in arrival(ND):
            go(h_copy(c, k))
    b.lsum[0] = total

    def loss_x(k):
        return send(b.lsum.at[0], b.lrec.at[k], b.l_sem, k, xdev((d + k) % ND))

    def loss_y(k):
        return send(b.lsum.at[1], b.lrec.at[ND + k], b.l_sem, ND + k, ydev((y + k) % NY))

    def loss_z():
        return send(b.lsum.at[2], b.lrec.at[ND + NY], b.l_sem, ND + NY, zdev)

    for k in range(1, ND):
        go(loss_x(k))

    def i_copy(c, rel):
        q = (y + rel) % NY
        return send(b.isend.at[c, q], b.irec.at[c, rel], b.i_sem, c * NY + rel, ydev(q))

    def iz_copy(c):
        return send(b.izsend.at[c], b.izrec.at[c], b.iz_sem, c, zdev)

    def i_step(c):
        for k in arrival(ND):
            h_copy(c, k).wait_recv()
        product(b.og, c, b.wout, b.isend, c, transposed=True)
        for rel in arrival(NY):
            go(i_copy(c, rel))

    def i_sum(c):
        for rel in range(1, NY):
            i_copy(c, rel).wait_recv()

        def total(cols):
            out = b.isend[c, y, :, cols].astype(F32)
            for rel in range(1, NY):
                out = out + b.irec[c, rel, :, cols].astype(F32)
            return out

        b.izsend[c] = total(half(oz)).astype(BF)
        go(iz_copy(c))
        b.grad[CR * c: CR * (c + 1), :] = total(half(zh))

    for c in range(NC):
        i_step(c)
        if c:
            i_sum(c - 1)
    total = b.lsum[0]
    for k in range(1, ND):
        loss_x(k).wait_recv()
        total = total + b.lrec[k]
    b.lsum[1] = total
    for k in range(1, NY):
        go(loss_y(k))
    i_sum(NC - 1)

    def store(n, carry):
        at = pl.ds(pl.multiple_of(n * 256, 256), 256)
        b.gout[at, :] = dot(b.mixt[at, :], b.og[...].reshape(ND * T, F)).astype(BF)
        return carry

    lax.fori_loop(0, C // 256, store, 0)
    total = b.lsum[1]
    for k in range(1, NY):
        loss_y(k).wait_recv()
        total = total + b.lrec[ND + k]
    b.lsum[2] = total
    go(loss_z())
    for c in range(NC):
        iz_copy(c).wait_recv()
        b.grad[CR * c: CR * (c + 1), :] += b.izrec[c].astype(F32)

    dscore = jnp.zeros((T, T), F32)
    sums = []
    at_lane = lax.broadcasted_iota(jnp.int32, (T, 128), 1)
    rowcols = jnp.zeros((T, 128), F32)
    for j in range(H // 128):
        cols = slice(128 * j, 128 * (j + 1))
        g = b.grad[:, cols]
        gb = g.astype(BF)
        v = b.vals[:, cols]
        prod = g * b.pure[:, cols]
        outs = []
        for e in (0, 1):
            k = 2 * j + e
            here = low if e == 0 else jnp.logical_not(low)
            x = dot(gb, jnp.where(here, v, 0.0).astype(BF), 1, 1)
            decay = b.decay[k]
            st = step[k: k + 1, :]
            xd = x * decay
            dscore = dscore + xd * st
            sums.append(jnp.sum(xd * scores, axis=0, keepdims=True))
            rowcols = jnp.where(
                at_lane == k, jnp.sum(jnp.where(here, prod, 0.0), axis=1, keepdims=True), rowcols
            )
            wt = (decay * scores * st).T.astype(BF)
            outs.append(dot(wt, gb))
        skips = jnp.where(low, b.skip[0, head0 + 2 * j], b.skip[0, head0 + 2 * j + 1])
        b.vg[:, y, :, lanes(j)] = (
            (jnp.where(low, outs[0], outs[1]) + skips * g).astype(BF).reshape(NC, CR, 128)
        )
    for c in range(NC):
        for rel in arrival(NY):
            go(spread_y(b.vg, b.k_sem, c, rel, 0))
    dstep = jnp.concatenate(sums, axis=0)
    dcum = rowcols.T[:HH, :] - step * dstep
    ddecay = dot(dcum, causal.astype(F32), precision=HI)
    draw = (dstep - rate * ddecay) * jax.nn.sigmoid(raw)
    drw = jnp.where(low, dot(dscore.T, wr, precision=HI), dot(dscore, wr, precision=HI)).T
    in_half = lax.broadcasted_iota(jnp.int32, (HB, T), 0) // HH == zh
    dsteps = jnp.where(in_half, jnp.concatenate([draw] * NZ, axis=0), 0.0)

    b.j1send[:W, :] = drw.astype(BF)
    b.j1send[W:, :] = dsteps.astype(BF)
    j1 = go(send(b.j1send, b.j1rec, b.iz_sem, NC, zdev))
    for c in range(NC):
        go(spread_z(b.vg, b.k_sem, c))
    j1.wait_recv()
    b.j2send[:W, :] = (drw + b.j1rec[:W, :].astype(F32)).astype(BF)
    b.j2send[W:, :] = (dsteps + b.j1rec[W:, :].astype(F32)).astype(BF)
    b.j2rec[d] = b.j2send[...]

    def j2_copy(k):
        return send(b.j2send, b.j2rec.at[d], b.j2_sem, k, xdev((d + k) % ND))

    for k in arrival(ND):
        go(j2_copy(k))
    spread_on(b.vg, b.k_sem)
    for k in arrival(ND):
        j2_copy(k).wait_recv()
    part = b.j2rec[0, :W, :].astype(F32)
    for q in range(1, ND):
        part = part + b.j2rec[q, :W, :].astype(F32)
    b.j3[y, :W, :] = part.astype(BF)
    for q in range(ND):
        b.j3[y, W + HB * q: W + HB * (q + 1), :] = b.j2rec[q, W:, :]

    def j3_copy(k):
        return send(b.j3.at[y], b.j3.at[y], b.j3_sem, k, ydev((y + k) % NY))

    for k in arrival(NY):
        go(j3_copy(k))
    loss_z().wait_recv()
    b.lout[...] = (
        jnp.zeros((8, 128), F32) + jnp.sum(b.lsum[2] + b.lrec[ND + NY]) / (T * ND * F * NY * NZ)
    )
    stores = []

    def write(src, dst):
        cp = pltpu.make_async_copy(src, dst, b.store_sem.at[len(stores)])
        cp.start()
        stores.append(cp)

    write(b.lout, loss)
    write(b.gout, g_out.at[0])
    for c in range(NC):
        spread_done(b.vg, b.k_sem, c)
    w = min(256, F)
    for n in range(F // w):
        b.gin[w * n: w * (n + 1), :] = dot(
            b.srct[w * n: w * (n + 1), :], b.vg[...].reshape(ND * T, C)
        ).astype(BF)
        write(b.gin.at[pl.ds(w * n, w)], g_in.at[0, pl.ds(w * n, w)])
    for k in arrival(NY):
        j3_copy(k).wait_recv()
    out = jnp.zeros((W + cfg.heads, F), F32)
    for q in range(NY):
        out = out + dot(b.j3[q], b.src[:, q].reshape(T, F))
    b.gside[...] = out.astype(BF)
    write(b.gside, g_side.at[0])

    finish()
    for cp in stores:
        cp.wait()


def local(states, final_state, retained, block_slot, w_in, w_side, w_out, a_rate, dt_bias, skip):
    nd, sec, nt = lax.axis_size("dp"), lax.axis_size("section"), lax.axis_size("tensor")
    ny = nt // NZ
    t, f = final_state.shape
    c = w_in.shape[2]
    heads = a_rate.shape[1]
    hb = c // P_SIZE
    sd = 2 * NS + heads
    side = 2 * NS + hb
    h = c // NZ
    n = t * nd
    nc = sec // 2
    cr = t // nc
    nstore = 3 + max(1, f // 256)
    assert ny == nd and t == 128
    V, S = pltpu.VMEM, pltpu.SMEM

    def sems(k):
        return pltpu.SemaphoreType.DMA((2, k))

    scratch = dict(
        retained=S((sec,), jnp.int32), slot=S((sec,), jnp.int32),
        rate=S((1, heads), F32), bias=S((1, heads), F32), skip=S((1, heads), F32),
        layers=V((2 * sec, t // sec, f), BF), stage=V((2, sec, t // sec, f), BF),
        src=V((nc, nd, cr, f), BF), tgt=V((t, f), BF), final=V((t, f), BF), srct=V((f, n), BF),
        win=V((f, c), BF), wside=V((sd, f), BF), wout=V((c, f), BF), wstep=V((hb, f), BF),
        psend=V((nc, ny, cr, c + 2 * NS), BF), prec=V((nc, ny, cr, c + 2 * NS), BF),
        zsend=V((nc, cr, h + 2 * NS), BF), zrec=V((nc, cr, h + 2 * NS), BF),
        stsend=V((ny, hb, t), BF), strec=V((ny, hb, t), BF), stz=V((2, hb, t), BF),
        steps=V((hb, t), F32), rw=V((t, 2 * NS), F32), vals=V((t, h), F32), pure=V((t, h), F32),
        decay=V((hb // NZ, t, t), F32), mix=V((nc, ny, cr, c), BF), mixt=V((c, n), BF),
        osend=V((nc, nd, cr, f), BF), orec=V((nc, nd, cr, f), BF), og=V((nc, nd, cr, f), BF),
        lsum=V((3, 8, 128), F32), lrec=V((nd + ny + 1, 8, 128), F32), lout=V((8, 128), F32),
        isend=V((nc, ny, cr, c), BF), irec=V((nc, ny, cr, c), BF),
        izsend=V((nc, cr, h), BF), izrec=V((nc, cr, h), BF), grad=V((t, h), F32),
        gout=V((c, f), BF), vg=V((nc, ny, cr, c), BF),
        j1send=V((side, t), BF), j1rec=V((side, t), BF),
        j2send=V((side, t), BF), j2rec=V((nd, side, t), BF), j3=V((ny, sd, t), BF),
        gin=V((f, c), BF), gside=V((sd, f), BF),
        load_sem=pltpu.SemaphoreType.DMA((10,)), store_sem=pltpu.SemaphoreType.DMA((nstore,)),
        h1_sem=sems(sec), h2_sem=sems(sec), h3_sem=sems(sec), g_sem=sems(nc * nd),
        c_sem=sems(nc * ny), z_sem=sems(nc), st_sem=sems(ny + 1), e_sem=sems(nc + 2 * nc * ny),
        f_sem=sems(nc * nd), h_sem=sems(nc * nd), i_sem=sems(nc * ny), iz_sem=sems(nc + 1),
        l_sem=sems(nd + ny + 1), k_sem=sems(nc + 2 * nc * ny), j2_sem=sems(nd), j3_sem=sems(ny),
    )
    cfg = SimpleNamespace(
        names=tuple(scratch), nd=nd, sec=sec, ny=ny, t=t, f=f, c=c, hb=hb, heads=heads
    )
    hbm = pl.BlockSpec(memory_space=pltpu.HBM)
    anywhere = pl.BlockSpec(memory_space=pl.ANY)
    g_in, g_side, g_out, loss = pl.pallas_call(
        functools.partial(kernel, cfg, None),
        out_shape=(
            jax.ShapeDtypeStruct(w_in.shape, BF), jax.ShapeDtypeStruct((1, sd, f), BF),
            jax.ShapeDtypeStruct(w_out.shape, BF), jax.ShapeDtypeStruct((8, 128), F32),
        ),
        in_specs=[hbm] * 10,
        out_specs=(anywhere,) * 4,
        scratch_shapes=list(scratch.values()),
        compiler_params=pltpu.CompilerParams(
            collective_id=0, has_side_effects=True, vmem_limit_bytes=36 << 20
        ),
        name="distill",
    )(
        states, final_state, retained, block_slot, w_in, jnp.swapaxes(w_side, 1, 2), w_out,
        a_rate, dt_bias, skip,
    )
    return g_in, jnp.swapaxes(g_side, 1, 2), g_out, loss[0, :1]


def solution(mesh):
    placed = (
        P("section", "dp", "tensor"),
        P("dp", "tensor"),
        P(),
        P(),
        P("section", "tensor", "dp"),
        P("section", "tensor", None),
        P("section", "dp", "tensor"),
        P("section", None),
        P("section", None),
        P("section", None),
    )
    return jax.shard_map(
        local,
        mesh=mesh,
        in_specs=placed,
        out_specs=(
            P("section", "tensor", "dp"),
            P("section", "tensor", None),
            P("section", "dp", "tensor"),
            P("section"),
        ),
        check_vma=False,
    )
```

```python
import functools
from types import SimpleNamespace

import jax
import jax.numpy as jnp
from jax import lax
from jax.experimental import pallas as pl
from jax.experimental.pallas import tpu as pltpu
from jax.sharding import PartitionSpec as P

P_SIZE = 64
NS = 64
VMEM_BYTES = 60 << 20
NZ = 2
MESH = pl.DeviceIdType.MESH
F32 = jnp.float32
BF = jnp.bfloat16
HI = lax.Precision.HIGHEST


def dot(a, b, ca=1, cb=0, precision=None):
    return lax.dot_general(
        a, b, (((ca,), (cb,)), ((), ())), preferred_element_type=F32, precision=precision
    )


class Copy:
    def __init__(self, copy, key, due):
        self.copy, self.key, self.due = copy, key, due
        self.start, self.wait_send = copy.start, copy.wait_send

    def wait_recv(self):
        self.copy.wait_recv()
        self.due.pop(self.key, None)


def arrival(n):
    return sorted(range(1, n), key=lambda k: min(k, n - k))


def kernel(cfg, stop, states, final, retained, slot, w_in, w_side, w_out, a_rate, dt_bias, skip,
           srct, vg, g_side, g_out, loss, *scratch):
    b = SimpleNamespace(**dict(zip(cfg.names, scratch)))
    ND, SEC, NY = cfg.nd, cfg.sec, cfg.ny
    T, F, C, H = cfg.t, cfg.f, cfg.c, cfg.c // NZ
    HB, HH = cfg.hb, cfg.hb // NZ
    NC = SEC // 2
    RC, CR = T // SEC, T // NC
    W = 2 * NS
    d, s, t = lax.axis_index("dp"), lax.axis_index("section"), lax.axis_index("tensor")
    zh, y = t // NY, t % NY
    oz = 1 - zh
    zl, core = s // 2, s % 2

    def xdev(i):
        return (i, s, t)

    def ydev(i):
        return (d, s, zh * NY + i)

    zdev = (d, s, oz * NY + y)

    if NC == 4:
        chips = [zl, zl + 1 - 2 * (zl % 2), (zl + 2) % 4, 3 - zl]
    else:
        chips = [zl, 1 - zl]
    sections = [2 * c + k for c in chips for k in (core, 1 - core)]
    far_first = [m for i in (2, 3, 1, 0) for m in (2 * i, 2 * i + 1) if 0 < m < SEC]

    def sdev(m):
        return (d, sections[m], t)

    bar = pltpu.get_barrier_semaphore()
    partners = (
        [sdev(m) for m in far_first]
        + [xdev((d + k) % ND) for k in range(1, ND)]
        + [ydev((y + k) % NY) for k in range(1, NY)]
        + [zdev]
    )
    for p in partners:
        pl.semaphore_signal(bar, inc=1, device_id=p, device_id_type=MESH)

    def rows(i, n):
        return pl.ds(pl.multiple_of(i * n, 16), n)

    def half(i):
        return pl.ds(pl.multiple_of(i * H, 128), H)

    PIECES = 2
    layers = (b.layers0, b.layers1)

    def piece(j):
        return pl.ds(j * (F // PIECES), F // PIECES)

    loads = [
        pltpu.make_async_copy(src, dst, b.load_sem.at[i])
        for i, (src, dst) in enumerate((
            (states.at[:, rows(s, RC), piece(0)], b.layers0.at[pl.ds(2 * s, 2)]),
            (states.at[:, rows(s, RC), piece(1)], b.layers1.at[pl.ds(2 * s, 2)]),
            (retained, b.retained), (slot, b.slot), (w_side.at[0], b.wside), (w_in.at[0], b.win.at[:, pl.ds(0, C)]),
            (a_rate, b.rate), (dt_bias, b.bias), (skip, b.skip), (w_out.at[0], b.wout), (final, b.final),
        ))
    ]
    for cp in loads:
        cp.start()
    loading = dict(enumerate(loads))

    def loaded(*which):
        for i in which:
            loading.pop(i).wait()

    def send(src, dst, sems, i, dev):
        cp = pltpu.make_async_remote_copy(
            src_ref=src, dst_ref=dst, send_sem=sems.at[0, i], recv_sem=sems.at[1, i],
            device_id=dev, device_id_type=MESH,
        )
        return Copy(cp, (id(sems), i), due)

    pending, due, stores = [], {}, []

    def write(src, dst):
        cp = pltpu.make_async_copy(src, dst, b.store_sem.at[len(stores)])
        cp.start()
        stores.append(cp)

    def go(cp):
        cp.start()
        pending.append(cp)
        due[cp.key] = cp
        return cp

    def finish():
        for cp in list(due.values()):
            cp.wait_recv()
        for i in list(loading):
            loaded(i)
        for cp in pending:
            cp.wait_send()
        for cp in stores:
            cp.wait()

    pl.semaphore_wait(bar, len(partners))

    hop1 = {}
    for j in range(PIECES):
        for m in far_first:
            hop1[j, m] = go(send(
                states.at[:, rows(sections[m], RC), piece(j)],
                layers[j].at[pl.ds(2 * s, 2)], b.h1_sem, j * SEC + m, sdev(m),
            ))
    loaded(0, 1, 2, 3, 4)
    wanted = []
    for i in range(SEC):
        layer = jnp.int32(0)
        for r in range(SEC):
            layer = layer + jnp.where(b.slot[r] == i, b.retained[r], 0)
        wanted.append(layer)

    def wanted_of(i):
        out = jnp.int32(0)
        for j in range(SEC):
            out = out + jnp.where(i == j, wanted[j], 0)
        return out

    layer_of = [wanted_of(i) for i in sections]
    pick = (
        lax.broadcasted_iota(jnp.int32, (HB, cfg.heads), 1)
        == lax.broadcasted_iota(jnp.int32, (HB, cfg.heads), 0) + d * HB
    )
    b.wstep[...] = dot(pick.astype(BF), b.wside[W:, :]).astype(BF)
    for j in range(F // 128):
        b.win[128 * j: 128 * (j + 1), C:] = b.wside[:W, 128 * j: 128 * (j + 1)].T
    loaded(9)
    for i in range(C // 128):
        for j in range(F // 128):
            b.woutt[128 * j: 128 * (j + 1), 128 * i: 128 * (i + 1)] = (
                b.wout[128 * i: 128 * (i + 1), 128 * j: 128 * (j + 1)].T
            )

    mine = rows(core, RC)
    hop2 = {}
    for j in range(PIECES):
        at = piece(j)
        for m in far_first:
            hop1[j, m].wait_recv()
        b.src[zl, d, mine, at] = layers[j][layer_of[0]]
        for m in range(1, SEC):
            b.stage[0, m, :, at] = layers[j][layer_of[m]]
            hop2[j, m] = go(send(
                b.stage.at[0, m, :, at], b.src.at[zl, d, mine, at], b.h2_sem, j * SEC + m, sdev(m)
            ))

    def g_copy(i, k):
        at = b.src.at[chips[i], d]
        return send(at, at, b.g_sem, i * ND + k, xdev((d + k) % ND))

    for i in range(NC):
        for m in (2 * i, 2 * i + 1):
            for j in range(PIECES if m else 0):
                hop2[j, m].wait_recv()
        for k in arrival(ND):
            go(g_copy(i, k))
    hop3 = []
    for m in range(1, SEC):
        for j in range(PIECES):
            b.stage[1, m, :, piece(j)] = layers[j][jnp.minimum(layer_of[m] + 1, 2 * SEC - 1)]
        hop3.append(go(send(b.stage.at[1, m], b.tgt.at[rows(s, RC)], b.h3_sem, m, sdev(m))))
    for j in range(PIECES):
        b.tgt[rows(s, RC), piece(j)] = layers[j][jnp.minimum(layer_of[0] + 1, 2 * SEC - 1)]
    loaded(5)

    def product(lhs, c, w, out, i):
        x = lhs[c].reshape(ND * CR, lhs.shape[3])
        out[i] = dot(x, w[...]).astype(BF).reshape(ND, CR, w.shape[1])

    def c_copy(i, rel):
        q = (y + rel) % NY
        return send(b.psend.at[i, q], b.prec.at[i, rel], b.c_sem, i * NY + rel, ydev(q))

    def z_copy(i):
        return send(b.zsend.at[i], b.zrec.at[i], b.z_sem, i, zdev)

    def c_step(i):
        for k in arrival(ND):
            g_copy(i, k).wait_recv()
        c = chips[i]
        product(b.src, c, b.win, b.psend, i)
        for rel in arrival(NY):
            go(c_copy(i, rel))

    def c_sum(i):
        for rel in range(1, NY):
            c_copy(i, rel).wait_recv()

        def total(cols):
            out = b.psend[i, y, :, cols].astype(F32)
            for rel in range(1, NY):
                out = out + b.prec[i, rel, :, cols].astype(F32)
            return out

        b.zsend[i, :, :H] = total(half(oz)).astype(BF)
        side = total(slice(C, C + W))
        b.zsend[i, :, H:] = side.astype(BF)
        go(z_copy(i))
        here = rows(chips[i], CR)
        b.vals[here, :] = total(half(zh))
        b.rw[here, :] = side

    def st_copy(rel):
        return send(b.stsend.at[rel], b.strec.at[rel], b.st_sem, rel, ydev((y + rel) % NY))

    for i in range(NC):
        c_step(i)
    for rel in arrival(NY) + [0]:
        x = b.src[:, (y + rel) % NY].reshape(T, F)
        b.stsend[rel] = dot(b.wstep[...], x, 1, 1).astype(BF)
        if rel:
            go(st_copy(rel))
    for c in range(NC):
        for j in range(F // 128):
            b.srct[128 * j: 128 * (j + 1), ND * CR * c: ND * CR * (c + 1)] = (
                b.src[c, :, :, 128 * j: 128 * (j + 1)].reshape(ND * CR, 128).T
            )
    write(b.srct, srct)
    for i in range(NC):
        c_sum(i)
    steps = b.stsend[0].astype(F32)
    for rel in range(1, NY):
        st_copy(rel).wait_recv()
        steps = steps + b.strec[rel].astype(F32)
    b.stz[0] = steps.astype(BF)
    stz = go(send(b.stz.at[0], b.stz.at[1], b.st_sem, NY, zdev))
    loaded(6, 7, 8)
    for i in range(NC):
        z_copy(i).wait_recv()
        here = rows(chips[i], CR)
        b.vals[here, :] += b.zrec[i, :, :H].astype(F32)
        b.rw[here, :] += b.zrec[i, :, H:].astype(F32)
    stz.wait_recv()
    b.steps[...] = steps + b.stz[1].astype(F32)

    head0 = d * HB + zh * HH

    def column(ref):
        at = lax.broadcasted_iota(jnp.int32, (HH, 1), 0)
        out = jnp.zeros((HH, 1), F32)
        for k in range(HH):
            out = jnp.where(at == k, ref[0, head0 + k], out)
        return out

    rate, bias = column(b.rate), column(b.bias)
    r_t = lax.broadcasted_iota(jnp.int32, (T, T), 0)
    r_u = lax.broadcasted_iota(jnp.int32, (T, T), 1)
    causal = r_t >= r_u
    low = r_u < NS
    raw = b.steps[pl.ds(pl.multiple_of(zh * HH, 8), HH), :] + bias
    step = jax.nn.softplus(raw)
    cum = dot(-(step * rate), (r_t <= r_u).astype(F32), precision=HI)
    rw = b.rw[...]
    wr = pltpu.roll(rw, NS, 1)
    scores = dot(jnp.where(low, wr, 0.0), rw, 1, 1, precision=HI)
    cum_cols = jnp.concatenate([cum] * (T // HH), axis=0).T
    for k in range(HH):
        diff = cum_cols[:, k: k + 1] - cum[k: k + 1, :]
        b.decay[k] = jnp.where(causal, jnp.exp(jnp.where(causal, diff, 0.0)), 0.0)

    def lanes(j):
        return pl.ds(pl.multiple_of(zh * H + 128 * j, 128), 128)

    for j in range(H // 128):
        cols = slice(128 * j, 128 * (j + 1))
        v = b.vals[:, cols]
        vb = v.astype(BF)
        outs = []
        for k in (2 * j, 2 * j + 1):
            w = (b.decay[k] * scores * step[k: k + 1, :]).astype(BF)
            outs.append(dot(w, vb))
        y2 = jnp.where(low, outs[0], outs[1])
        b.pure[:, cols] = y2
        skips = jnp.where(low, b.skip[0, head0 + 2 * j], b.skip[0, head0 + 2 * j + 1])
        b.mix[:, y, :, lanes(j)] = (y2 + skips * v).astype(BF).reshape(NC, CR, 128)

    def spread_z(buf, sems, c):
        at = buf.at[c, y, :, half(zh)]
        return send(at, at, sems, c, zdev)

    def spread_y(buf, sems, c, rel, which):
        at = buf.at[c, y, :, half(oz if which else zh)]
        return send(at, at, sems, NC + (2 * c + which) * NY + rel, ydev((y + rel) % NY))

    def spread(buf, sems):
        for c in range(NC):
            go(spread_z(buf, sems, c))
            for rel in arrival(NY):
                go(spread_y(buf, sems, c, rel, 0))

    def spread_on(buf, sems):
        for c in range(NC):
            spread_z(buf, sems, c).wait_recv()
            for rel in arrival(NY):
                go(spread_y(buf, sems, c, rel, 1))

    def spread_done(buf, sems, c):
        for rel in arrival(NY):
            for which in (0, 1):
                spread_y(buf, sems, c, rel, which).wait_recv()

    spread(b.mix, b.e_sem)
    spread_on(b.mix, b.e_sem)

    def f_copy(c, rel):
        q = (d + rel) % ND
        return send(b.osend.at[c, q], b.orec.at[c, rel], b.f_sem, c * ND + rel, xdev(q))

    for c in range(NC):
        spread_done(b.mix, b.e_sem, c)
        product(b.mix, c, b.wout, b.osend, c)
        for rel in arrival(ND):
            go(f_copy(c, rel))
    for c in range(NC):
        for j in range(C // 128):
            b.mixt[128 * j: 128 * (j + 1), NY * CR * c: NY * CR * (c + 1)] = (
                b.mix[c, :, :, 128 * j: 128 * (j + 1)].reshape(NY * CR, 128).T
            )
    loaded(10)
    for cp in hop3:
        cp.wait_recv()
    inner = layer_of[0] + 1 < 2 * SEC

    def h_copy(c, k):
        at = b.og.at[c, d]
        return send(at, at, b.h_sem, c * ND + k, xdev((d + k) % ND))

    total = jnp.zeros((8, 128), F32)
    for c in range(NC):
        for rel in range(1, ND):
            f_copy(c, rel).wait_recv()
        for j in range(F // 128):
            cols = slice(128 * j, 128 * (j + 1))
            here = slice(CR * c, CR * (c + 1))
            out = b.osend[c, d, :, cols].astype(F32)
            for rel in range(1, ND):
                out = out + b.orec[c, rel, :, cols].astype(F32)
            goal = jnp.where(inner, b.tgt[here, cols].astype(F32), b.final[here, cols].astype(F32))
            err = out - goal
            b.og[c, d, :, cols] = (2.0 * err / (T * ND)).astype(BF)
            total = total + jnp.sum((err * err).reshape(CR // 8, 8, 128), axis=0)
        for k in arrival(ND):
            go(h_copy(c, k))
    b.lsum[0] = total

    def loss_x(k):
        return send(b.lsum.at[0], b.lrec.at[k], b.l_sem, k, xdev((d + k) % ND))

    def loss_y(k):
        return send(b.lsum.at[1], b.lrec.at[ND + k], b.l_sem, ND + k, ydev((y + k) % NY))

    def loss_z():
        return send(b.lsum.at[2], b.lrec.at[ND + NY], b.l_sem, ND + NY, zdev)

    for k in range(1, ND):
        go(loss_x(k))

    def i_copy(c, rel):
        q = (y + rel) % NY
        return send(b.isend.at[c, q], b.irec.at[c, rel], b.i_sem, c * NY + rel, ydev(q))

    def iz_copy(c):
        return send(b.izsend.at[c], b.izrec.at[c], b.iz_sem, c, zdev)

    def i_step(c):
        for k in arrival(ND):
            h_copy(c, k).wait_recv()
        product(b.og, c, b.woutt, b.isend, c)
        for rel in arrival(NY):
            go(i_copy(c, rel))

    def i_sum(c):
        for rel in range(1, NY):
            i_copy(c, rel).wait_recv()

        def total(cols):
            out = b.isend[c, y, :, cols].astype(F32)
            for rel in range(1, NY):
                out = out + b.irec[c, rel, :, cols].astype(F32)
            return out

        b.izsend[c] = total(half(oz)).astype(BF)
        go(iz_copy(c))
        b.grad[CR * c: CR * (c + 1), :] = total(half(zh))

    for c in range(NC):
        i_step(c)
    total = b.lsum[0]
    for k in range(1, ND):
        loss_x(k).wait_recv()
        total = total + b.lrec[k]
    b.lsum[1] = total
    for k in range(1, NY):
        go(loss_y(k))
    for c in range(NC):
        i_sum(c)
    for n in range(C // 256):
        at = slice(256 * n, 256 * (n + 1))
        b.gout[at, :] = dot(b.mixt[at, :], b.og[...].reshape(ND * T, F)).astype(BF)
    write(b.gout, g_out)
    total = b.lsum[1]
    for k in range(1, NY):
        loss_y(k).wait_recv()
        total = total + b.lrec[ND + k]
    b.lsum[2] = total
    go(loss_z())
    for c in range(NC):
        iz_copy(c).wait_recv()
        b.grad[CR * c: CR * (c + 1), :] += b.izrec[c].astype(F32)

    def k_lanes(j, own):
        return pl.ds(pl.multiple_of((zh if own else oz) * H + 128 * j, 128), 128)

    def k_z(j):
        at = b.vg.at[:, y, :, k_lanes(j, True)]
        return send(at, at, b.k_sem, j, zdev)

    def k_y(j, rel, which):
        at = b.vg.at[:, y, :, k_lanes(j, not which)]
        return send(at, at, b.k_sem, NJ + (2 * j + which) * NY + rel, ydev((y + rel) % NY))

    NJ = H // 128
    dscore = jnp.zeros((T, T), F32)
    sums = []
    at_lane = lax.broadcasted_iota(jnp.int32, (T, 128), 1)
    rowcols = jnp.zeros((T, 128), F32)
    for j in range(H // 128):
        cols = slice(128 * j, 128 * (j + 1))
        g = b.grad[:, cols]
        gb = g.astype(BF)
        v = b.vals[:, cols]
        prod = g * b.pure[:, cols]
        outs = []
        for e in (0, 1):
            k = 2 * j + e
            here = low if e == 0 else jnp.logical_not(low)
            x = dot(gb, jnp.where(here, v, 0.0).astype(BF), 1, 1)
            decay = b.decay[k]
            st = step[k: k + 1, :]
            xd = x * decay
            dscore = dscore + xd * st
            sums.append(jnp.sum(xd * scores, axis=0, keepdims=True))
            rowcols = jnp.where(
                at_lane == k, jnp.sum(jnp.where(here, prod, 0.0), axis=1, keepdims=True), rowcols
            )
            wt = (decay * scores * st).T.astype(BF)
            outs.append(dot(wt, gb))
        skips = jnp.where(low, b.skip[0, head0 + 2 * j], b.skip[0, head0 + 2 * j + 1])
        b.vg[:, y, :, lanes(j)] = (
            (jnp.where(low, outs[0], outs[1]) + skips * g).astype(BF).reshape(NC, CR, 128)
        )
        go(k_z(j))
        for rel in arrival(NY):
            go(k_y(j, rel, 0))
    dstep = jnp.concatenate(sums, axis=0)
    dcum = rowcols.T[:HH, :] - step * dstep
    ddecay = dot(dcum, causal.astype(F32), precision=HI)
    draw = (dstep - rate * ddecay) * jax.nn.sigmoid(raw)
    drw = jnp.where(low, dot(dscore.T, wr, precision=HI), dot(dscore, wr, precision=HI)).T
    in_half = lax.broadcasted_iota(jnp.int32, (HB, T), 0) // HH == zh
    dsteps = jnp.where(in_half, jnp.concatenate([draw] * NZ, axis=0), 0.0)

    b.j1send[:W, :] = drw.astype(BF)
    b.j1send[W:, :] = dsteps.astype(BF)
    j1 = go(send(b.j1send, b.j1rec, b.iz_sem, NC, zdev))
    j1.wait_recv()
    b.j2send[:W, :] = (drw + b.j1rec[:W, :].astype(F32)).astype(BF)
    b.j2send[W:, :] = (dsteps + b.j1rec[W:, :].astype(F32)).astype(BF)
    b.j2rec[d] = b.j2send[...]

    def j2_copy(k):
        return send(b.j2send, b.j2rec.at[d], b.j2_sem, k, xdev((d + k) % ND))

    for k in arrival(ND):
        go(j2_copy(k))
    for j in range(NJ):
        k_z(j).wait_recv()
        for rel in arrival(NY):
            go(k_y(j, rel, 1))
    for k in arrival(ND):
        j2_copy(k).wait_recv()
    part = b.j2rec[0, :W, :].astype(F32)
    for q in range(1, ND):
        part = part + b.j2rec[q, :W, :].astype(F32)
    b.j3[y, :W, :] = part.astype(BF)
    for q in range(ND):
        b.j3[y, W + HB * q: W + HB * (q + 1), :] = b.j2rec[q, W:, :]

    def j3_copy(k):
        return send(b.j3.at[y], b.j3.at[y], b.j3_sem, k, ydev((y + k) % NY))

    for k in arrival(NY):
        go(j3_copy(k))
    loss_z().wait_recv()
    b.lout[...] = (
        jnp.zeros((8, 128), F32) + jnp.sum(b.lsum[2] + b.lrec[ND + NY]) / (T * ND * F * NY * NZ)
    )
    write(b.lout, loss)
    for j in range(NJ):
        for rel in arrival(NY):
            for which in (0, 1):
                k_y(j, rel, which).wait_recv()
        for h in range(NZ):
            at = pl.ds(h * H + 128 * j, 128)
            write(b.vg.at[:, :, :, at], vg.at[:, :, :, at])
    for k in arrival(NY):
        j3_copy(k).wait_recv()
    out = jnp.zeros((W + cfg.heads, F), F32)
    for q in range(NY):
        out = out + dot(b.j3[q], b.src[:, q].reshape(T, F))
    b.gside[...] = out.astype(BF)
    write(b.gside, g_side)

    finish()


def last(srct, vg, side, out, loss, g_in, g_side, g_out, mean,
         left, right, rows, means, sides, outs, sems):
    n, block = rows.shape[0], rows.shape[1]
    fetch = [
        pltpu.make_async_copy(a, z, sems.at[i])
        for i, (a, z) in enumerate((
            (srct, left), (vg, right), (loss, means), (side, sides), (out, outs)
        ))
    ]
    store = [
        pltpu.make_async_copy(a, z.at[0], sems.at[len(fetch) + i])
        for i, (a, z) in enumerate(((outs, g_out), (sides, g_side)))
    ]
    for cp in fetch:
        cp.start()
    for cp in fetch[:3]:
        cp.wait()
    mean[0] = jnp.max(means[...])
    for i in range(n):
        x = left[block * i: block * (i + 1), :]
        rows[i] = dot(x, right[...].reshape(left.shape[1], right.shape[3])).astype(BF)
        if i == 0:
            fetch[4].wait()
            store[0].start()
            fetch[3].wait()
            store[1].start()
        cp = pltpu.make_async_copy(
            rows.at[i], g_in.at[0, pl.ds(block * i, block)], sems.at[len(fetch) + 2 + i]
        )
        cp.start()
        store.append(cp)
    for cp in store:
        cp.wait()


def local(states, final_state, retained, block_slot, w_in, w_side, w_out, a_rate, dt_bias, skip):
    nd, sec, nt = lax.axis_size("dp"), lax.axis_size("section"), lax.axis_size("tensor")
    ny = nt // NZ
    t, f = final_state.shape
    c = w_in.shape[2]
    heads = a_rate.shape[1]
    hb = c // P_SIZE
    sd = 2 * NS + heads
    side = 2 * NS + hb
    h = c // NZ
    n = t * nd
    nc = sec // 2
    cr = t // nc
    nstore = 4 + c // 128
    assert ny == nd and t == 128
    V, S = pltpu.VMEM, pltpu.SMEM

    def sems(k):
        return pltpu.SemaphoreType.DMA((2, k))

    scratch = dict(
        retained=S((sec,), jnp.int32), slot=S((sec,), jnp.int32),
        rate=S((1, heads), F32), bias=S((1, heads), F32), skip=S((1, heads), F32),
        layers0=V((2 * sec, t // sec, f // 2), BF), layers1=V((2 * sec, t // sec, f // 2), BF), stage=V((2, sec, t // sec, f), BF),
        src=V((nc, nd, cr, f), BF), tgt=V((t, f), BF), final=V((t, f), BF), srct=V((f, n), BF),
        win=V((f, c + 2 * NS), BF), woutt=V((f, c), BF), wside=V((sd, f), BF), wout=V((c, f), BF), wstep=V((hb, f), BF),
        psend=V((nc, ny, cr, c + 2 * NS), BF), prec=V((nc, ny, cr, c + 2 * NS), BF),
        zsend=V((nc, cr, h + 2 * NS), BF), zrec=V((nc, cr, h + 2 * NS), BF),
        stsend=V((ny, hb, t), BF), strec=V((ny, hb, t), BF), stz=V((2, hb, t), BF),
        steps=V((hb, t), F32), rw=V((t, 2 * NS), F32), vals=V((t, h), F32), pure=V((t, h), F32),
        decay=V((hb // NZ, t, t), F32), mix=V((nc, ny, cr, c), BF), mixt=V((c, n), BF),
        osend=V((nc, nd, cr, f), BF), orec=V((nc, nd, cr, f), BF), og=V((nc, nd, cr, f), BF),
        lsum=V((3, 8, 128), F32), lrec=V((nd + ny + 1, 8, 128), F32), lout=V((8, 128), F32),
        isend=V((nc, ny, cr, c), BF), irec=V((nc, ny, cr, c), BF),
        izsend=V((nc, cr, h), BF), izrec=V((nc, cr, h), BF), grad=V((t, h), F32),
        gout=V((c, f), BF), vg=V((nc, ny, cr, c), BF),
        j1send=V((side, t), BF), j1rec=V((side, t), BF),
        j2send=V((side, t), BF), j2rec=V((nd, side, t), BF), j3=V((ny, sd, t), BF),
        gside=V((sd, f), BF),
        load_sem=pltpu.SemaphoreType.DMA((11,)), store_sem=pltpu.SemaphoreType.DMA((nstore,)),
        h1_sem=sems(2 * sec), h2_sem=sems(2 * sec), h3_sem=sems(sec), g_sem=sems(nc * nd),
        c_sem=sems(nc * ny), z_sem=sems(nc), st_sem=sems(ny + 1), e_sem=sems(nc + 2 * nc * ny),
        f_sem=sems(nc * nd), h_sem=sems(nc * nd), i_sem=sems(nc * ny), iz_sem=sems(nc + 1),
        l_sem=sems(nd + ny + 1), k_sem=sems(h // 128 * (1 + 2 * ny)), j2_sem=sems(nd), j3_sem=sems(ny),
    )
    cfg = SimpleNamespace(
        names=tuple(scratch), nd=nd, sec=sec, ny=ny, t=t, f=f, c=c, hb=hb, heads=heads
    )
    hbm = pl.BlockSpec(memory_space=pl.ANY)
    shape = jax.ShapeDtypeStruct
    parts = pl.pallas_call(
        functools.partial(kernel, cfg, None),
        out_shape=(
            shape((f, n), BF), shape((nc, ny, cr, c), BF), shape((sd, f), BF), shape((c, f), BF),
            shape((8, 128), F32),
        ),
        in_specs=[hbm] * 10,
        out_specs=(hbm,) * 5,
        scratch_shapes=list(scratch.values()),
        compiler_params=pltpu.CompilerParams(
            collective_id=0, has_side_effects=True, vmem_limit_bytes=VMEM_BYTES
        ),
        name="distill",
    )(
        states, final_state, retained, block_slot, w_in, jnp.swapaxes(w_side, 1, 2), w_out,
        a_rate, dt_bias, skip,
    )
    block = min(256, f)
    g_in, g_side, g_out, mean = pl.pallas_call(
        last,
        out_shape=(
            shape(w_in.shape, BF), shape((1, sd, f), BF), shape(w_out.shape, BF), shape((1,), F32)
        ),
        in_specs=[hbm] * 5,
        out_specs=(hbm, hbm, hbm, pl.BlockSpec(memory_space=S)),
        scratch_shapes=[
            V((f, n), BF), V((nc, ny, cr, c), BF), V((f // block, block, c), BF), V((8, 128), F32),
            V((sd, f), BF), V((c, f), BF), pltpu.SemaphoreType.DMA((7 + f // block,)),
        ],
        compiler_params=pltpu.CompilerParams(vmem_limit_bytes=VMEM_BYTES),
        name="last",
    )(*parts)
    return g_in, jnp.swapaxes(g_side, 1, 2), g_out, mean


def solution(mesh):
    placed = (
        P("section", "dp", "tensor"),
        P("dp", "tensor"),
        P(),
        P(),
        P("section", "tensor", "dp"),
        P("section", "tensor", None),
        P("section", "dp", "tensor"),
        P("section", None),
        P("section", None),
        P("section", None),
    )
    return jax.shard_map(
        local,
        mesh=mesh,
        in_specs=placed,
        out_specs=(
            P("section", "tensor", "dp"),
            P("section", "tensor", None),
            P("section", "dp", "tensor"),
            P("section"),
        ),
        check_vma=False,
    )
```

```python
import functools
from types import SimpleNamespace

import jax
import jax.numpy as jnp
from jax import lax
from jax.experimental import pallas as pl
from jax.experimental.pallas import tpu as pltpu
from jax.sharding import PartitionSpec as P

P_SIZE = 64
NS = 64
VMEM_BYTES = 60 << 20
CHUNKS = (4, 8)
LAGS = (4, 8, 8, 8)
NZ = 2
MESH = pl.DeviceIdType.MESH
F32 = jnp.float32
BF = jnp.bfloat16
HI = lax.Precision.HIGHEST


def dot(a, b, ca=1, cb=0, precision=None):
    return lax.dot_general(
        a, b, (((ca,), (cb,)), ((), ())), preferred_element_type=F32, precision=precision
    )


class Copy:
    def __init__(self, copy, key, due):
        self.copy, self.key, self.due = copy, key, due
        self.start, self.wait_send = copy.start, copy.wait_send

    def wait_recv(self):
        self.copy.wait_recv()
        self.due.pop(self.key, None)


def arrival(n):
    return sorted(range(1, n), key=lambda k: min(k, n - k))


def kernel(cfg, stop, states, final, retained, slot, w_in, w_side, w_out, a_rate, dt_bias, skip,
           g_in, g_side, g_out, loss, *scratch):
    b = SimpleNamespace(**dict(zip(cfg.names, scratch)))
    ND, SEC, NY = cfg.nd, cfg.sec, cfg.ny
    T, F, C, H = cfg.t, cfg.f, cfg.c, cfg.c // NZ
    HB, HH = cfg.hb, cfg.hb // NZ
    NA, NB = cfg.na, cfg.nb
    RC, CA, CB = T // SEC, T // NA, T // NB
    PC = SEC // NA
    W = 2 * NS
    d, s, t = lax.axis_index("dp"), lax.axis_index("section"), lax.axis_index("tensor")
    zh, y = t // NY, t % NY
    oz = 1 - zh
    zl, core = s // 2, s % 2

    def xdev(i):
        return (i, s, t)

    def ydev(i):
        return (d, s, zh * NY + i)

    zdev = (d, s, oz * NY + y)

    if SEC == 8:
        chips = [zl, zl + 1 - 2 * (zl % 2), (zl + 2) % 4, 3 - zl]
    else:
        chips = [zl, 1 - zl]
    sections = [2 * c + k for c in chips for k in (core, 1 - core)]
    chunks = [i // PC for i in sections[::PC]]
    far_first = [m for i in (2, 3, 1, 0) for m in (2 * i, 2 * i + 1) if 0 < m < SEC]

    def sdev(m):
        return (d, sections[m], t)

    bar = pltpu.get_barrier_semaphore()
    partners = (
        [sdev(m) for m in far_first]
        + [xdev((d + k) % ND) for k in range(1, ND)]
        + [ydev((y + k) % NY) for k in range(1, NY)]
        + [zdev]
    )
    for p in partners:
        pl.semaphore_signal(bar, inc=1, device_id=p, device_id_type=MESH)

    def rows(i, n):
        return pl.ds(pl.multiple_of(i * n, 16), n)

    def half(i):
        return pl.ds(pl.multiple_of(i * H, 128), H)

    PIECES = 2
    layers = (b.layers0, b.layers1)

    def piece(j):
        return pl.ds(j * (F // PIECES), F // PIECES)

    loads = [
        pltpu.make_async_copy(src, dst, b.load_sem.at[i])
        for i, (src, dst) in enumerate((
            (states.at[:, rows(s, RC), piece(0)], b.layers0.at[pl.ds(2 * s, 2)]),
            (states.at[:, rows(s, RC), piece(1)], b.layers1.at[pl.ds(2 * s, 2)]),
            (retained, b.retained), (slot, b.slot), (w_side.at[0], b.wside), (w_in.at[0], b.win.at[:, pl.ds(0, C)]),
            (a_rate, b.rate), (dt_bias, b.bias), (skip, b.skip), (w_out.at[0], b.wout), (final, b.final),
        ))
    ]
    for cp in loads:
        cp.start()
    loading = dict(enumerate(loads))

    def loaded(*which):
        for i in which:
            loading.pop(i).wait()

    def send(src, dst, sems, i, dev):
        cp = pltpu.make_async_remote_copy(
            src_ref=src, dst_ref=dst, send_sem=sems.at[0, i], recv_sem=sems.at[1, i],
            device_id=dev, device_id_type=MESH,
        )
        return Copy(cp, (id(sems), i), due)

    pending, due, stores = [], {}, []

    def write(src, dst):
        cp = pltpu.make_async_copy(src, dst, b.store_sem.at[len(stores)])
        cp.start()
        stores.append(cp)

    def go(cp):
        cp.start()
        pending.append(cp)
        due[cp.key] = cp
        return cp

    def finish():
        for cp in list(due.values()):
            cp.wait_recv()
        for i in list(loading):
            loaded(i)
        for cp in pending:
            cp.wait_send()
        for cp in stores:
            cp.wait()

    pl.semaphore_wait(bar, len(partners))

    hop1 = {}
    for j in range(PIECES):
        for m in far_first:
            hop1[j, m] = go(send(
                states.at[:, rows(sections[m], RC), piece(j)],
                layers[j].at[pl.ds(2 * s, 2)], b.h1_sem, j * SEC + m, sdev(m),
            ))
    loaded(0, 1, 2, 3, 4)
    wanted = []
    for i in range(SEC):
        layer = jnp.int32(0)
        for r in range(SEC):
            layer = layer + jnp.where(b.slot[r] == i, b.retained[r], 0)
        wanted.append(layer)

    def wanted_of(i):
        out = jnp.int32(0)
        for j in range(SEC):
            out = out + jnp.where(i == j, wanted[j], 0)
        return out

    layer_of = [wanted_of(i) for i in sections]
    pick = (
        lax.broadcasted_iota(jnp.int32, (HB, cfg.heads), 1)
        == lax.broadcasted_iota(jnp.int32, (HB, cfg.heads), 0) + d * HB
    )
    b.wstep[...] = dot(pick.astype(BF), b.wside[W:, :]).astype(BF)
    for j in range(F // 128):
        b.win[128 * j: 128 * (j + 1), C:] = b.wside[:W, 128 * j: 128 * (j + 1)].T
    loaded(9)
    for i in range(C // 128):
        for j in range(F // 128):
            b.woutt[128 * j: 128 * (j + 1), 128 * i: 128 * (i + 1)] = (
                b.wout[128 * i: 128 * (i + 1), 128 * j: 128 * (j + 1)].T
            )

    mine = rows(s % PC, RC)
    hop2 = {}
    for j in range(PIECES):
        at = piece(j)
        for m in far_first:
            hop1[j, m].wait_recv()
        b.src[s // PC, d, mine, at] = layers[j][layer_of[0]]
        for m in range(1, SEC):
            b.stage[0, m, :, at] = layers[j][layer_of[m]]
            hop2[j, m] = go(send(
                b.stage.at[0, m, :, at], b.src.at[s // PC, d, mine, at], b.h2_sem, j * SEC + m, sdev(m)
            ))

    def g_copy(i, k):
        at = b.src.at[chunks[i], d]
        return send(at, at, b.g_sem, i * ND + k, xdev((d + k) % ND))

    for i in range(NA):
        for m in range(PC * i, PC * (i + 1)):
            for j in range(PIECES if m else 0):
                hop2[j, m].wait_recv()
        for k in arrival(ND):
            go(g_copy(i, k))
    hop3 = []
    for m in range(1, SEC):
        for j in range(PIECES):
            b.stage[1, m, :, piece(j)] = layers[j][jnp.minimum(layer_of[m] + 1, 2 * SEC - 1)]
        hop3.append(go(send(b.stage.at[1, m], b.tgt.at[rows(s, RC)], b.h3_sem, m, sdev(m))))
    for j in range(PIECES):
        b.tgt[rows(s, RC), piece(j)] = layers[j][jnp.minimum(layer_of[0] + 1, 2 * SEC - 1)]
    loaded(5)

    def product(lhs, c, w, out, i):
        x = lhs[c].reshape(ND * lhs.shape[2], lhs.shape[3])
        out[i] = dot(x, w[...]).astype(BF).reshape(ND, lhs.shape[2], w.shape[1])

    def c_copy(i, rel):
        q = (y + rel) % NY
        return send(b.psend.at[i, q], b.prec.at[i, rel], b.c_sem, i * NY + rel, ydev(q))

    def z_copy(i):
        return send(b.zsend.at[i], b.zrec.at[i], b.z_sem, i, zdev)

    def c_step(i):
        for k in arrival(ND):
            g_copy(i, k).wait_recv()
        c = chunks[i]
        product(b.src, c, b.win, b.psend, i)
        for rel in arrival(NY):
            go(c_copy(i, rel))

    def c_sum(i):
        for rel in range(1, NY):
            c_copy(i, rel).wait_recv()

        def total(cols):
            out = b.psend[i, y, :, cols].astype(F32)
            for rel in range(1, NY):
                out = out + b.prec[i, rel, :, cols].astype(F32)
            return out

        b.zsend[i, :, :H] = total(half(oz)).astype(BF)
        side = total(slice(C, C + W))
        b.zsend[i, :, H:] = side.astype(BF)
        go(z_copy(i))
        here = rows(chunks[i], CA)
        b.vals[here, :] = total(half(zh))
        b.rw[here, :] = side

    def st_copy(rel):
        return send(b.stsend.at[rel], b.strec.at[rel], b.st_sem, rel, ydev((y + rel) % NY))

    for i in range(NA - 1 + LAGS[0]):
        if i < NA:
            c_step(i)
        if 0 <= i - LAGS[0] < NA - 1:
            c_sum(i - LAGS[0])
    for rel in arrival(NY) + [0]:
        x = b.src[:, (y + rel) % NY].reshape(T, F)
        b.stsend[rel] = dot(b.wstep[...], x, 1, 1).astype(BF)
        if rel:
            go(st_copy(rel))
    c_sum(NA - 1)
    steps = b.stsend[0].astype(F32)
    for rel in range(1, NY):
        st_copy(rel).wait_recv()
        steps = steps + b.strec[rel].astype(F32)
    b.stz[0] = steps.astype(BF)
    stz = go(send(b.stz.at[0], b.stz.at[1], b.st_sem, NY, zdev))
    loaded(6, 7, 8)
    for i in range(NA):
        z_copy(i).wait_recv()
        here = rows(chunks[i], CA)
        b.vals[here, :] += b.zrec[i, :, :H].astype(F32)
        b.rw[here, :] += b.zrec[i, :, H:].astype(F32)
    stz.wait_recv()
    b.steps[...] = steps + b.stz[1].astype(F32)

    head0 = d * HB + zh * HH

    def column(ref):
        at = lax.broadcasted_iota(jnp.int32, (HH, 1), 0)
        out = jnp.zeros((HH, 1), F32)
        for k in range(HH):
            out = jnp.where(at == k, ref[0, head0 + k], out)
        return out

    rate, bias = column(b.rate), column(b.bias)
    r_t = lax.broadcasted_iota(jnp.int32, (T, T), 0)
    r_u = lax.broadcasted_iota(jnp.int32, (T, T), 1)
    causal = r_t >= r_u
    low = r_u < NS
    raw = b.steps[pl.ds(pl.multiple_of(zh * HH, 8), HH), :] + bias
    step = jax.nn.softplus(raw)
    cum = dot(-(step * rate), (r_t <= r_u).astype(F32), precision=HI)
    rw = b.rw[...]
    wr = pltpu.roll(rw, NS, 1)
    scores = dot(jnp.where(low, wr, 0.0), rw, 1, 1, precision=HI)
    cum_cols = jnp.concatenate([cum] * (T // HH), axis=0).T
    for k in range(HH):
        diff = cum_cols[:, k: k + 1] - cum[k: k + 1, :]
        b.decay[k] = jnp.where(causal, jnp.exp(jnp.where(causal, diff, 0.0)), 0.0)

    def lanes(j):
        return pl.ds(pl.multiple_of(zh * H + 128 * j, 128), 128)

    for j in range(H // 128):
        cols = slice(128 * j, 128 * (j + 1))
        v = b.vals[:, cols]
        vb = v.astype(BF)
        outs = []
        for k in (2 * j, 2 * j + 1):
            w = (b.decay[k] * scores * step[k: k + 1, :]).astype(BF)
            outs.append(dot(w, vb))
        y2 = jnp.where(low, outs[0], outs[1])
        b.pure[:, cols] = y2
        skips = jnp.where(low, b.skip[0, head0 + 2 * j], b.skip[0, head0 + 2 * j + 1])
        b.mix[:, y, :, lanes(j)] = (y2 + skips * v).astype(BF).reshape(NB, CB, 128)

    def spread_z(buf, sems, c):
        at = buf.at[c, y, :, half(zh)]
        return send(at, at, sems, c, zdev)

    def spread_y(buf, sems, c, rel, which):
        at = buf.at[c, y, :, half(oz if which else zh)]
        return send(at, at, sems, NB + (2 * c + which) * NY + rel, ydev((y + rel) % NY))

    def spread(buf, sems):
        for c in range(NB):
            go(spread_z(buf, sems, c))
            for rel in arrival(NY):
                go(spread_y(buf, sems, c, rel, 0))

    def spread_on(buf, sems):
        for c in range(NB):
            spread_z(buf, sems, c).wait_recv()
            for rel in arrival(NY):
                go(spread_y(buf, sems, c, rel, 1))

    def spread_done(buf, sems, c):
        for rel in arrival(NY):
            for which in (0, 1):
                spread_y(buf, sems, c, rel, which).wait_recv()

    spread(b.mix, b.e_sem)
    spread_on(b.mix, b.e_sem)

    def f_copy(c, rel):
        q = (d + rel) % ND
        return send(b.osend.at[c, q], b.orec.at[c, rel], b.f_sem, c * ND + rel, xdev(q))

    inner = layer_of[0] + 1 < 2 * SEC

    def h_copy(c, k):
        at = b.og.at[c, d]
        return send(at, at, b.h_sem, c * ND + k, xdev((d + k) % ND))


    def loss_x(k):
        return send(b.lsum.at[0], b.lrec.at[k], b.l_sem, k, xdev((d + k) % ND))

    def loss_y(k):
        return send(b.lsum.at[1], b.lrec.at[ND + k], b.l_sem, ND + k, ydev((y + k) % NY))

    def loss_z():
        return send(b.lsum.at[2], b.lrec.at[ND + NY], b.l_sem, ND + NY, zdev)

    def i_copy(c, rel):
        q = (y + rel) % NY
        return send(b.isend.at[c, q], b.irec.at[c, rel], b.i_sem, c * NY + rel, ydev(q))

    def iz_copy(c):
        return send(b.izsend.at[c], b.izrec.at[c], b.iz_sem, c, zdev)

    def i_step(c):
        for k in arrival(ND):
            h_copy(c, k).wait_recv()
        product(b.og, c, b.woutt, b.isend, c)
        for rel in arrival(NY):
            go(i_copy(c, rel))

    def i_sum(c):
        for rel in range(1, NY):
            i_copy(c, rel).wait_recv()

        def total(cols):
            out = b.isend[c, y, :, cols].astype(F32)
            for rel in range(1, NY):
                out = out + b.irec[c, rel, :, cols].astype(F32)
            return out

        b.izsend[c] = total(half(oz)).astype(BF)
        go(iz_copy(c))
        b.grad[CB * c: CB * (c + 1), :] = total(half(zh))

    def f_step(c):
        spread_done(b.mix, b.e_sem, c)
        product(b.mix, c, b.wout, b.osend, c)
        for rel in arrival(ND):
            go(f_copy(c, rel))

    def err_step(c):
        total = jnp.zeros((8, 128), F32)
        for rel in range(1, ND):
            f_copy(c, rel).wait_recv()
        for j in range(F // 128):
            cols = slice(128 * j, 128 * (j + 1))
            here = slice(CB * c, CB * (c + 1))
            out = b.osend[c, d, :, cols].astype(F32)
            for rel in range(1, ND):
                out = out + b.orec[c, rel, :, cols].astype(F32)
            goal = jnp.where(inner, b.tgt[here, cols].astype(F32), b.final[here, cols].astype(F32))
            err = out - goal
            b.og[c, d, :, cols] = (2.0 * err / (T * ND)).astype(BF)
            total = total + jnp.sum((err * err).reshape(CB // 8, 8, 128), axis=0)
        for k in arrival(ND):
            go(h_copy(c, k))
        return total

    def prepare():
        for c in range(NB):
            for j in range(C // 128):
                b.mixt[128 * j: 128 * (j + 1), NY * CB * c: NY * CB * (c + 1)] = (
                    b.mix[c, :, :, 128 * j: 128 * (j + 1)].reshape(NY * CB, 128).T
                )
        for c in range(NA):
            for j in range(F // 128):
                b.srct[128 * j: 128 * (j + 1), ND * CA * c: ND * CA * (c + 1)] = (
                    b.src[c, :, :, 128 * j: 128 * (j + 1)].reshape(ND * CA, 128).T
                )
        for k in range(HH):
            decay, st = b.decay[k], step[k: k + 1, :]
            both = decay * scores
            b.both[k] = both
            b.wt[k] = (both * st).T.astype(BF)
            b.decay[k] = decay * st
            cols = slice(128 * (k // 2), 128 * (k // 2 + 1))
            b.vmask[k] = jnp.where(low if k % 2 == 0 else jnp.logical_not(low), b.vals[:, cols], 0.0).astype(BF)

    loaded(10)
    for cp in hop3:
        cp.wait_recv()
    total = jnp.zeros((8, 128), F32)
    order = tuple(min(k, NB) for k in LAGS[1:])
    for i in range(NB + sum(order)):
        if i < NB:
            f_step(i)
        if i == NB - 1:
            prepare()
        if 0 <= i - order[0] < NB:
            total = total + err_step(i - order[0])
        if i - order[0] == NB - 1:
            b.lsum[0] = total
            for k in range(1, ND):
                go(loss_x(k))
        if 0 <= i - sum(order[:2]) < NB:
            i_step(i - sum(order[:2]))
        if 0 <= i - sum(order) < NB:
            i_sum(i - sum(order))
    total = b.lsum[0]
    for k in range(1, ND):
        loss_x(k).wait_recv()
        total = total + b.lrec[k]
    b.lsum[1] = total
    for k in range(1, NY):
        go(loss_y(k))
    for n in range(C // 256):
        at = slice(256 * n, 256 * (n + 1))
        b.gout[at, :] = dot(b.mixt[at, :], b.og[...].reshape(ND * T, F)).astype(BF)
    write(b.gout, g_out)
    total = b.lsum[1]
    for k in range(1, NY):
        loss_y(k).wait_recv()
        total = total + b.lrec[ND + k]
    b.lsum[2] = total
    go(loss_z())
    for c in range(NB):
        iz_copy(c).wait_recv()
        b.grad[CB * c: CB * (c + 1), :] += b.izrec[c].astype(F32)

    def k_lanes(j, own):
        return pl.ds(pl.multiple_of((zh if own else oz) * H + 128 * j, 128), 128)

    def k_z(j):
        at = b.vg.at[:, y, :, k_lanes(j, True)]
        return send(at, at, b.k_sem, j, zdev)

    def k_y(j, rel, which):
        at = b.vg.at[:, y, :, k_lanes(j, not which)]
        return send(at, at, b.k_sem, NJ + (2 * j + which) * NY + rel, ydev((y + rel) % NY))

    NJ = H // 128
    for j in range(H // 128):
        cols = slice(128 * j, 128 * (j + 1))
        g = b.grad[:, cols]
        gb = g.astype(BF)
        outs = [dot(b.wt[2 * j + e], gb) for e in (0, 1)]
        skips = jnp.where(low, b.skip[0, head0 + 2 * j], b.skip[0, head0 + 2 * j + 1])
        b.vg[:, y, :, lanes(j)] = (
            (jnp.where(low, outs[0], outs[1]) + skips * g).astype(BF).reshape(NA, CA, 128)
        )
        go(k_z(j))
        for rel in arrival(NY):
            go(k_y(j, rel, 0))
    dscore = jnp.zeros((T, T), F32)
    sums = []
    at_lane = lax.broadcasted_iota(jnp.int32, (T, 128), 1)
    rowcols = jnp.zeros((T, 128), F32)
    for j in range(H // 128):
        cols = slice(128 * j, 128 * (j + 1))
        g = b.grad[:, cols]
        gb = g.astype(BF)
        prod = g * b.pure[:, cols]
        for e in (0, 1):
            k = 2 * j + e
            here = low if e == 0 else jnp.logical_not(low)
            x = dot(gb, b.vmask[k], 1, 1)
            dscore = dscore + x * b.decay[k]
            sums.append(jnp.sum(x * b.both[k], axis=0, keepdims=True))
            rowcols = jnp.where(
                at_lane == k, jnp.sum(jnp.where(here, prod, 0.0), axis=1, keepdims=True), rowcols
            )
    dstep = jnp.concatenate(sums, axis=0)
    dcum = rowcols.T[:HH, :] - step * dstep
    ddecay = dot(dcum, causal.astype(F32), precision=HI)
    wrb = wr.astype(BF)
    draw = (dstep - rate * ddecay) * jax.nn.sigmoid(raw)
    drw = jnp.where(low, dot(dscore.T.astype(BF), wrb), dot(dscore.astype(BF), wrb)).T
    in_half = lax.broadcasted_iota(jnp.int32, (HB, T), 0) // HH == zh
    dsteps = jnp.where(in_half, jnp.concatenate([draw] * NZ, axis=0), 0.0)

    b.j1send[:W, :] = drw.astype(BF)
    b.j1send[W:, :] = dsteps.astype(BF)
    j1 = go(send(b.j1send, b.j1rec, b.iz_sem, NB, zdev))
    for j in range(NJ):
        k_z(j).wait_recv()
        for rel in arrival(NY):
            go(k_y(j, rel, 1))
    j1.wait_recv()
    b.j2send[:W, :] = (drw + b.j1rec[:W, :].astype(F32)).astype(BF)
    b.j2send[W:, :] = (dsteps + b.j1rec[W:, :].astype(F32)).astype(BF)
    b.j2rec[d] = b.j2send[...]

    def j2_copy(k):
        return send(b.j2send, b.j2rec.at[d], b.j2_sem, k, xdev((d + k) % ND))

    for k in arrival(ND):
        go(j2_copy(k))
    for k in arrival(ND):
        j2_copy(k).wait_recv()
    part = b.j2rec[0, :W, :].astype(F32)
    for q in range(1, ND):
        part = part + b.j2rec[q, :W, :].astype(F32)
    b.j3[y, :W, :] = part.astype(BF)
    for q in range(ND):
        b.j3[y, W + HB * q: W + HB * (q + 1), :] = b.j2rec[q, W:, :]

    def j3_copy(k):
        return send(b.j3.at[y], b.j3.at[y], b.j3_sem, k, ydev((y + k) % NY))

    for k in arrival(NY):
        go(j3_copy(k))
    loss_z().wait_recv()
    b.lout[...] = (
        jnp.zeros((8, 128), F32) + jnp.sum(b.lsum[2] + b.lrec[ND + NY]) / (T * ND * F * NY * NZ)
    )
    write(b.lout, loss)
    for j in range(NJ):
        for rel in arrival(NY):
            for which in (0, 1):
                k_y(j, rel, which).wait_recv()
        halves = [slice(h * H + 128 * j, h * H + 128 * (j + 1)) for h in range(NZ)]
        vg = jnp.concatenate([b.vg[:, :, :, at].reshape(ND * T, 128) for at in halves], axis=1)
        part = dot(b.srct[...], vg).astype(BF)
        for h, at in enumerate(halves):
            b.gin[:, at] = part[:, 128 * h: 128 * (h + 1)]
            write(b.gin.at[:, at], g_in.at[:, at])
    for k in arrival(NY):
        j3_copy(k).wait_recv()
    out = jnp.zeros((W + cfg.heads, F), F32)
    for q in range(NY):
        out = out + dot(b.j3[q], b.src[:, q].reshape(T, F))
    b.gside[...] = out.astype(BF)
    write(b.gside, g_side)

    finish()


def last(side, out, inn, loss, g_side, g_out, g_in, mean, sides, outs, inns, means, sems):
    moves = []
    for a, v, z in ((out, outs, g_out), (inn, inns, g_in), (side, sides, g_side)):
        n = a.shape[0]
        size = max(n // 4, 64)
        for i in range(n // size):
            moves.append((a, v, z, pl.ds(size * i, size)))
    fetch = [
        pltpu.make_async_copy(a.at[at], v.at[at], sems.at[0, i])
        for i, (a, v, z, at) in enumerate(moves)
    ]
    store = [
        pltpu.make_async_copy(v.at[at], z.at[0, at], sems.at[1, i])
        for i, (a, v, z, at) in enumerate(moves)
    ]
    whole = pltpu.make_async_copy(loss, means, sems.at[0, len(moves)])
    for cp in fetch + [whole]:
        cp.start()
    for f, z in zip(fetch, store):
        f.wait()
        z.start()
    whole.wait()
    mean[0] = jnp.max(means[...])
    for cp in store:
        cp.wait()


def local(states, final_state, retained, block_slot, w_in, w_side, w_out, a_rate, dt_bias, skip):
    nd, sec, nt = lax.axis_size("dp"), lax.axis_size("section"), lax.axis_size("tensor")
    ny = nt // NZ
    t, f = final_state.shape
    c = w_in.shape[2]
    heads = a_rate.shape[1]
    hb = c // P_SIZE
    sd = 2 * NS + heads
    sr = 2 * NS + hb
    h = c // NZ
    n = t * nd
    na, nb = min(CHUNKS[0], sec), CHUNKS[1]
    ca, cb = t // na, t // nb
    nstore = 3 + c // 128
    assert ny == nd and t == 128
    V, S = pltpu.VMEM, pltpu.SMEM

    def sems(k):
        return pltpu.SemaphoreType.DMA((2, k))

    scratch = dict(
        retained=S((sec,), jnp.int32), slot=S((sec,), jnp.int32),
        rate=S((1, heads), F32), bias=S((1, heads), F32), skip=S((1, heads), F32),
        layers0=V((2 * sec, t // sec, f // 2), BF), layers1=V((2 * sec, t // sec, f // 2), BF), stage=V((2, sec, t // sec, f), BF),
        src=V((na, nd, ca, f), BF), tgt=V((t, f), BF), final=V((t, f), BF), srct=V((f, n), BF),
        win=V((f, c + 2 * NS), BF), woutt=V((f, c), BF), wside=V((sd, f), BF), wout=V((c, f), BF), wstep=V((hb, f), BF),
        psend=V((na, ny, ca, c + 2 * NS), BF), prec=V((na, ny, ca, c + 2 * NS), BF),
        zsend=V((na, ca, h + 2 * NS), BF), zrec=V((na, ca, h + 2 * NS), BF),
        stsend=V((ny, hb, t), BF), strec=V((ny, hb, t), BF), stz=V((2, hb, t), BF),
        steps=V((hb, t), F32), rw=V((t, 2 * NS), F32), vals=V((t, h), F32), pure=V((t, h), F32),
        decay=V((hb // NZ, t, t), F32), both=V((hb // NZ, t, t), F32),
        wt=V((hb // NZ, t, t), BF), vmask=V((hb // NZ, t, t), BF), mix=V((nb, ny, cb, c), BF), mixt=V((c, n), BF),
        osend=V((nb, nd, cb, f), BF), orec=V((nb, nd, cb, f), BF), og=V((nb, nd, cb, f), BF),
        lsum=V((3, 8, 128), F32), lrec=V((nd + ny + 1, 8, 128), F32), lout=V((8, 128), F32),
        isend=V((nb, ny, cb, c), BF), irec=V((nb, ny, cb, c), BF),
        izsend=V((nb, cb, h), BF), izrec=V((nb, cb, h), BF), grad=V((t, h), F32),
        gout=V((c, f), BF), gin=V((f, c), BF), vg=V((na, ny, ca, c), BF),
        j1send=V((sr, t), BF), j1rec=V((sr, t), BF),
        j2send=V((sr, t), BF), j2rec=V((nd, sr, t), BF), j3=V((ny, sd, t), BF),
        gside=V((sd, f), BF),
        load_sem=pltpu.SemaphoreType.DMA((11,)), store_sem=pltpu.SemaphoreType.DMA((nstore,)),
        h1_sem=sems(2 * sec), h2_sem=sems(2 * sec), h3_sem=sems(sec), g_sem=sems(na * nd),
        c_sem=sems(na * ny), z_sem=sems(na), st_sem=sems(ny + 1), e_sem=sems(nb + 2 * nb * ny),
        f_sem=sems(nb * nd), h_sem=sems(nb * nd), i_sem=sems(nb * ny), iz_sem=sems(nb + 1),
        l_sem=sems(nd + ny + 1), k_sem=sems(h // 128 * (1 + 2 * ny)), j2_sem=sems(nd), j3_sem=sems(ny),
    )
    cfg = SimpleNamespace(
        names=tuple(scratch), nd=nd, sec=sec, ny=ny, t=t, f=f, c=c, hb=hb, heads=heads, na=na, nb=nb
    )
    hbm = pl.BlockSpec(memory_space=pl.ANY)
    shape = jax.ShapeDtypeStruct
    inn, side, out, loss = pl.pallas_call(
        functools.partial(kernel, cfg, None),
        out_shape=(
            shape((f, c), BF), shape((sd, f), BF), shape((c, f), BF), shape((8, 128), F32),
        ),
        in_specs=[hbm] * 10,
        out_specs=(hbm,) * 4,
        scratch_shapes=list(scratch.values()),
        compiler_params=pltpu.CompilerParams(
            collective_id=0, has_side_effects=True, vmem_limit_bytes=VMEM_BYTES
        ),
        name="distill",
    )(
        states, final_state, retained, block_slot, w_in, jnp.swapaxes(w_side, 1, 2), w_out,
        a_rate, dt_bias, skip,
    )
    g_side, g_out, g_in, mean = pl.pallas_call(
        last,
        out_shape=(
            shape((1, sd, f), BF), shape(w_out.shape, BF), shape(w_in.shape, BF), shape((1,), F32)
        ),
        in_specs=[hbm] * 4,
        out_specs=(hbm, hbm, hbm, pl.BlockSpec(memory_space=S)),
        scratch_shapes=[
            V((sd, f), BF), V((c, f), BF), V((f, c), BF), V((8, 128), F32),
            pltpu.SemaphoreType.DMA((2, 16)),
        ],
        compiler_params=pltpu.CompilerParams(vmem_limit_bytes=VMEM_BYTES),
        name="last",
    )(side, out, inn, loss)
    return g_in, jnp.swapaxes(g_side, 1, 2), g_out, mean


def solution(mesh):
    placed = (
        P("section", "dp", "tensor"),
        P("dp", "tensor"),
        P(),
        P(),
        P("section", "tensor", "dp"),
        P("section", "tensor", None),
        P("section", "dp", "tensor"),
        P("section", None),
        P("section", None),
        P("section", None),
    )
    return jax.shard_map(
        local,
        mesh=mesh,
        in_specs=placed,
        out_specs=(
            P("section", "tensor", "dp"),
            P("section", "tensor", None),
            P("section", "dp", "tensor"),
            P("section"),
        ),
        check_vma=False,
    )
```

```python
import functools
from types import SimpleNamespace

import jax
import jax.numpy as jnp
from jax import lax
from jax.experimental import pallas as pl
from jax.experimental.pallas import tpu as pltpu
from jax.sharding import PartitionSpec as P

P_SIZE = 64
NS = 64
VMEM_BYTES = 60 << 20
CHUNKS = (4, 8)
LAGS = (4, 8, 8, 8)
NZ = 2
MESH = pl.DeviceIdType.MESH
F32 = jnp.float32
BF = jnp.bfloat16
HI = lax.Precision.HIGHEST


def dot(a, b, ca=1, cb=0, precision=None):
    return lax.dot_general(
        a, b, (((ca,), (cb,)), ((), ())), preferred_element_type=F32, precision=precision
    )


class Copy:
    def __init__(self, copy, key, due):
        self.copy, self.key, self.due = copy, key, due
        self.start, self.wait_send = copy.start, copy.wait_send

    def wait_recv(self):
        self.copy.wait_recv()
        self.due.pop(self.key, None)


def arrival(n):
    return sorted(range(1, n), key=lambda k: min(k, n - k))


def kernel(cfg, stop, states, final, retained, slot, w_in, w_side, w_out, a_rate, dt_bias, skip,
           g_in, g_side, g_out, loss, *scratch):
    b = SimpleNamespace(**dict(zip(cfg.names, scratch)))
    ND, SEC, NY = cfg.nd, cfg.sec, cfg.ny
    T, F, C, H = cfg.t, cfg.f, cfg.c, cfg.c // NZ
    HB, HH = cfg.hb, cfg.hb // NZ
    NA, NB = cfg.na, cfg.nb
    RC, CA, CB = T // SEC, T // NA, T // NB
    PC = SEC // NA
    W = 2 * NS
    d, s, t = lax.axis_index("dp"), lax.axis_index("section"), lax.axis_index("tensor")
    zh, y = t // NY, t % NY
    oz = 1 - zh
    zl, core = s // 2, s % 2

    def xdev(i):
        return (i, s, t)

    def ydev(i):
        return (d, s, zh * NY + i)

    zdev = (d, s, oz * NY + y)

    if SEC == 8:
        chips = [zl, zl + 1 - 2 * (zl % 2), (zl + 2) % 4, 3 - zl]
    else:
        chips = [zl, 1 - zl]
    sections = [2 * c + k for c in chips for k in (core, 1 - core)]
    chunks = [i // PC for i in sections[::PC]]
    far_first = [m for i in (2, 3, 1, 0) for m in (2 * i, 2 * i + 1) if 0 < m < SEC]

    def sdev(m):
        return (d, sections[m], t)

    bar = pltpu.get_barrier_semaphore()
    partners = (
        [sdev(m) for m in far_first]
        + [xdev((d + k) % ND) for k in range(1, ND)]
        + [ydev((y + k) % NY) for k in range(1, NY)]
        + [zdev]
    )
    for p in partners:
        pl.semaphore_signal(bar, inc=1, device_id=p, device_id_type=MESH)

    def rows(i, n):
        return pl.ds(pl.multiple_of(i * n, 16), n)

    def half(i):
        return pl.ds(pl.multiple_of(i * H, 128), H)

    PIECES = 2
    layers = (b.layers0, b.layers1)

    def piece(j):
        return pl.ds(j * (F // PIECES), F // PIECES)

    loads = [
        pltpu.make_async_copy(src, dst, b.load_sem.at[i])
        for i, (src, dst) in enumerate((
            (states.at[:, rows(s, RC), piece(0)], b.layers0.at[pl.ds(2 * s, 2)]),
            (states.at[:, rows(s, RC), piece(1)], b.layers1.at[pl.ds(2 * s, 2)]),
            (retained, b.retained), (slot, b.slot), (w_side.at[0], b.wside), (w_in.at[0], b.win.at[:, pl.ds(0, C)]),
            (a_rate, b.rate), (dt_bias, b.bias), (skip, b.skip), (w_out.at[0], b.wout), (final, b.final),
        ))
    ]
    for cp in loads:
        cp.start()
    loading = dict(enumerate(loads))

    def loaded(*which):
        for i in which:
            loading.pop(i).wait()

    def send(src, dst, sems, i, dev):
        cp = pltpu.make_async_remote_copy(
            src_ref=src, dst_ref=dst, send_sem=sems.at[0, i], recv_sem=sems.at[1, i],
            device_id=dev, device_id_type=MESH,
        )
        return Copy(cp, (id(sems), i), due)

    pending, due, stores = [], {}, []

    def write(src, dst):
        cp = pltpu.make_async_copy(src, dst, b.store_sem.at[len(stores)])
        cp.start()
        stores.append(cp)

    def go(cp):
        cp.start()
        pending.append(cp)
        due[cp.key] = cp
        return cp

    def finish():
        for cp in list(due.values()):
            cp.wait_recv()
        for i in list(loading):
            loaded(i)
        for cp in pending:
            cp.wait_send()
        for cp in stores:
            cp.wait()

    pl.semaphore_wait(bar, len(partners))

    hop1 = {}
    for j in range(PIECES):
        for m in far_first:
            hop1[j, m] = go(send(
                states.at[:, rows(sections[m], RC), piece(j)],
                layers[j].at[pl.ds(2 * s, 2)], b.h1_sem, j * SEC + m, sdev(m),
            ))
    loaded(0, 1, 2, 3, 4)
    wanted = []
    for i in range(SEC):
        layer = jnp.int32(0)
        for r in range(SEC):
            layer = layer + jnp.where(b.slot[r] == i, b.retained[r], 0)
        wanted.append(layer)

    def wanted_of(i):
        out = jnp.int32(0)
        for j in range(SEC):
            out = out + jnp.where(i == j, wanted[j], 0)
        return out

    layer_of = [wanted_of(i) for i in sections]
    pick = (
        lax.broadcasted_iota(jnp.int32, (HB, cfg.heads), 1)
        == lax.broadcasted_iota(jnp.int32, (HB, cfg.heads), 0) + d * HB
    )
    b.wstep[...] = dot(pick.astype(BF), b.wside[W:, :]).astype(BF)
    for j in range(F // 128):
        b.win[128 * j: 128 * (j + 1), C:] = b.wside[:W, 128 * j: 128 * (j + 1)].T
    loaded(9)
    for i in range(C // 128):
        for j in range(F // 128):
            b.woutt[128 * j: 128 * (j + 1), 128 * i: 128 * (i + 1)] = (
                b.wout[128 * i: 128 * (i + 1), 128 * j: 128 * (j + 1)].T
            )

    mine = rows(s % PC, RC)
    hop2 = {}
    for j in range(PIECES):
        at = piece(j)
        for m in far_first:
            hop1[j, m].wait_recv()
        b.src[s // PC, d, mine, at] = layers[j][layer_of[0]]
        for m in range(1, SEC):
            b.stage[0, m, :, at] = layers[j][layer_of[m]]
            hop2[j, m] = go(send(
                b.stage.at[0, m, :, at], b.src.at[s // PC, d, mine, at], b.h2_sem, j * SEC + m, sdev(m)
            ))

    def g_copy(i, k):
        at = b.src.at[chunks[i], d]
        return send(at, at, b.g_sem, i * ND + k, xdev((d + k) % ND))

    for i in range(NA):
        for m in range(PC * i, PC * (i + 1)):
            for j in range(PIECES if m else 0):
                hop2[j, m].wait_recv()
        for k in arrival(ND):
            go(g_copy(i, k))
    hop3 = []
    for m in range(1, SEC):
        for j in range(PIECES):
            b.stage[1, m, :, piece(j)] = layers[j][jnp.minimum(layer_of[m] + 1, 2 * SEC - 1)]
        hop3.append(go(send(b.stage.at[1, m], b.tgt.at[rows(s, RC)], b.h3_sem, m, sdev(m))))
    for j in range(PIECES):
        b.tgt[rows(s, RC), piece(j)] = layers[j][jnp.minimum(layer_of[0] + 1, 2 * SEC - 1)]
    loaded(5)

    def product(lhs, c, w, out, i):
        x = lhs[c].reshape(ND * lhs.shape[2], lhs.shape[3])
        out[i] = dot(x, w[...]).astype(BF).reshape(ND, lhs.shape[2], w.shape[1])

    def c_copy(i, rel):
        q = (y + rel) % NY
        return send(b.psend.at[i, q], b.prec.at[i, rel], b.c_sem, i * NY + rel, ydev(q))

    def z_copy(i):
        return send(b.zsend.at[i], b.zrec.at[i], b.z_sem, i, zdev)

    def c_step(i):
        for k in arrival(ND):
            g_copy(i, k).wait_recv()
        c = chunks[i]
        product(b.src, c, b.win, b.psend, i)
        for rel in arrival(NY):
            go(c_copy(i, rel))

    def c_sum(i):
        for rel in range(1, NY):
            c_copy(i, rel).wait_recv()

        def total(cols):
            out = b.psend[i, y, :, cols].astype(F32)
            for rel in range(1, NY):
                out = out + b.prec[i, rel, :, cols].astype(F32)
            return out

        b.zsend[i, :, :H] = total(half(oz)).astype(BF)
        side = total(slice(C, C + W))
        b.zsend[i, :, H:] = side.astype(BF)
        go(z_copy(i))
        here = rows(chunks[i], CA)
        b.vals[here, :] = total(half(zh))
        b.rw[here, :] = side

    def st_copy(rel):
        return send(b.stsend.at[rel], b.strec.at[rel], b.st_sem, rel, ydev((y + rel) % NY))

    for i in range(NA - 1 + LAGS[0]):
        if i < NA:
            c_step(i)
        if 0 <= i - LAGS[0] < NA - 1:
            c_sum(i - LAGS[0])
    for rel in arrival(NY) + [0]:
        x = b.src[:, (y + rel) % NY].reshape(T, F)
        b.stsend[rel] = dot(b.wstep[...], x, 1, 1).astype(BF)
        if rel:
            go(st_copy(rel))
    c_sum(NA - 1)
    steps = b.stsend[0].astype(F32)
    for rel in range(1, NY):
        st_copy(rel).wait_recv()
        steps = steps + b.strec[rel].astype(F32)
    b.stz[0] = steps.astype(BF)
    stz = go(send(b.stz.at[0], b.stz.at[1], b.st_sem, NY, zdev))
    loaded(6, 7, 8)
    for i in range(NA):
        z_copy(i).wait_recv()
        here = rows(chunks[i], CA)
        b.vals[here, :] += b.zrec[i, :, :H].astype(F32)
        b.rw[here, :] += b.zrec[i, :, H:].astype(F32)
    stz.wait_recv()
    b.steps[...] = steps + b.stz[1].astype(F32)

    head0 = d * HB + zh * HH

    def column(ref):
        at = lax.broadcasted_iota(jnp.int32, (HH, 1), 0)
        out = jnp.zeros((HH, 1), F32)
        for k in range(HH):
            out = jnp.where(at == k, ref[0, head0 + k], out)
        return out

    rate, bias = column(b.rate), column(b.bias)
    r_t = lax.broadcasted_iota(jnp.int32, (T, T), 0)
    r_u = lax.broadcasted_iota(jnp.int32, (T, T), 1)
    causal = r_t >= r_u
    low = r_u < NS
    raw = b.steps[pl.ds(pl.multiple_of(zh * HH, 8), HH), :] + bias
    step = jax.nn.softplus(raw)
    cum = dot(-(step * rate), (r_t <= r_u).astype(F32), precision=HI)
    rw = b.rw[...]
    wr = pltpu.roll(rw, NS, 1)
    scores = dot(jnp.where(low, wr, 0.0), rw, 1, 1, precision=HI)
    cum_cols = jnp.concatenate([cum] * (T // HH), axis=0).T
    for k in range(HH):
        diff = cum_cols[:, k: k + 1] - cum[k: k + 1, :]
        b.decay[k] = jnp.where(causal, jnp.exp(jnp.where(causal, diff, 0.0)), 0.0)

    def lanes(j):
        return pl.ds(pl.multiple_of(zh * H + 128 * j, 128), 128)

    for j in range(H // 128):
        cols = slice(128 * j, 128 * (j + 1))
        v = b.vals[:, cols]
        vb = v.astype(BF)
        outs = []
        for k in (2 * j, 2 * j + 1):
            w = (b.decay[k] * scores * step[k: k + 1, :]).astype(BF)
            outs.append(dot(w, vb))
        y2 = jnp.where(low, outs[0], outs[1])
        b.pure[:, cols] = y2
        skips = jnp.where(low, b.skip[0, head0 + 2 * j], b.skip[0, head0 + 2 * j + 1])
        b.mix[:, y, :, lanes(j)] = (y2 + skips * v).astype(BF).reshape(NB, CB, 128)

    def spread_z(buf, sems, c):
        at = buf.at[c, y, :, half(zh)]
        return send(at, at, sems, c, zdev)

    def spread_y(buf, sems, c, rel, which):
        at = buf.at[c, y, :, half(oz if which else zh)]
        return send(at, at, sems, NB + (2 * c + which) * NY + rel, ydev((y + rel) % NY))

    def spread(buf, sems):
        for c in range(NB):
            go(spread_z(buf, sems, c))
        for c in range(NB):
            for rel in arrival(NY):
                go(spread_y(buf, sems, c, rel, 0))

    def spread_on(buf, sems):
        for c in range(NB):
            spread_z(buf, sems, c).wait_recv()
            for rel in arrival(NY):
                go(spread_y(buf, sems, c, rel, 1))

    def spread_done(buf, sems, c):
        for rel in arrival(NY):
            for which in (0, 1):
                spread_y(buf, sems, c, rel, which).wait_recv()

    spread(b.mix, b.e_sem)
    spread_on(b.mix, b.e_sem)

    def f_copy(c, rel):
        q = (d + rel) % ND
        return send(b.osend.at[c, q], b.orec.at[c, rel], b.f_sem, c * ND + rel, xdev(q))

    inner = layer_of[0] + 1 < 2 * SEC

    def h_copy(c, k):
        at = b.og.at[c, d]
        return send(at, at, b.h_sem, c * ND + k, xdev((d + k) % ND))


    def loss_x(k):
        return send(b.lsum.at[0], b.lrec.at[k], b.l_sem, k, xdev((d + k) % ND))

    def loss_y(k):
        return send(b.lsum.at[1], b.lrec.at[ND + k], b.l_sem, ND + k, ydev((y + k) % NY))

    def loss_z():
        return send(b.lsum.at[2], b.lrec.at[ND + NY], b.l_sem, ND + NY, zdev)

    def i_copy(c, rel):
        q = (y + rel) % NY
        return send(b.isend.at[c, q], b.irec.at[c, rel], b.i_sem, c * NY + rel, ydev(q))

    def iz_copy(c):
        return send(b.izsend.at[c], b.izrec.at[c], b.iz_sem, c, zdev)

    def i_step(c):
        for k in arrival(ND):
            h_copy(c, k).wait_recv()
        product(b.og, c, b.woutt, b.isend, c)
        for rel in arrival(NY):
            go(i_copy(c, rel))

    def i_sum(c):
        for rel in range(1, NY):
            i_copy(c, rel).wait_recv()

        def total(cols):
            out = b.isend[c, y, :, cols].astype(F32)
            for rel in range(1, NY):
                out = out + b.irec[c, rel, :, cols].astype(F32)
            return out

        b.izsend[c] = total(half(oz)).astype(BF)
        go(iz_copy(c))
        b.grad[CB * c: CB * (c + 1), :] = total(half(zh))

    def f_step(c):
        spread_done(b.mix, b.e_sem, c)
        product(b.mix, c, b.wout, b.osend, c)
        for rel in arrival(ND):
            go(f_copy(c, rel))

    def err_step(c):
        total = jnp.zeros((8, 128), F32)
        for rel in range(1, ND):
            f_copy(c, rel).wait_recv()
        for j in range(F // 128):
            cols = slice(128 * j, 128 * (j + 1))
            here = slice(CB * c, CB * (c + 1))
            out = b.osend[c, d, :, cols].astype(F32)
            for rel in range(1, ND):
                out = out + b.orec[c, rel, :, cols].astype(F32)
            goal = jnp.where(inner, b.tgt[here, cols].astype(F32), b.final[here, cols].astype(F32))
            err = out - goal
            b.og[c, d, :, cols] = (2.0 * err / (T * ND)).astype(BF)
            total = total + jnp.sum((err * err).reshape(CB // 8, 8, 128), axis=0)
        for k in arrival(ND):
            go(h_copy(c, k))
        return total

    def prepare():
        for c in range(NB):
            for j in range(C // 128):
                b.mixt[128 * j: 128 * (j + 1), NY * CB * c: NY * CB * (c + 1)] = (
                    b.mix[c, :, :, 128 * j: 128 * (j + 1)].reshape(NY * CB, 128).T
                )
        for c in range(NA):
            for j in range(F // 128):
                b.srct[128 * j: 128 * (j + 1), ND * CA * c: ND * CA * (c + 1)] = (
                    b.src[c, :, :, 128 * j: 128 * (j + 1)].reshape(ND * CA, 128).T
                )
        for k in range(HH):
            decay, st = b.decay[k], step[k: k + 1, :]
            both = decay * scores
            b.both[k] = both
            b.wt[k] = (both * st).T.astype(BF)
            b.decay[k] = decay * st
            cols = slice(128 * (k // 2), 128 * (k // 2 + 1))
            b.vmask[k] = jnp.where(low if k % 2 == 0 else jnp.logical_not(low), b.vals[:, cols], 0.0).astype(BF)

    loaded(10)
    for cp in hop3:
        cp.wait_recv()
    total = jnp.zeros((8, 128), F32)
    order = tuple(min(k, NB) for k in LAGS[1:])
    for i in range(NB + sum(order)):
        if i < NB:
            f_step(i)
        if i == NB - 1:
            prepare()
        if 0 <= i - order[0] < NB:
            total = total + err_step(i - order[0])
        if i - order[0] == NB - 1:
            b.lsum[0] = total
            for k in range(1, ND):
                go(loss_x(k))
        if 0 <= i - sum(order[:2]) < NB:
            i_step(i - sum(order[:2]))
        if 0 <= i - sum(order) < NB:
            i_sum(i - sum(order))
    total = b.lsum[0]
    for k in range(1, ND):
        loss_x(k).wait_recv()
        total = total + b.lrec[k]
    b.lsum[1] = total
    for k in range(1, NY):
        go(loss_y(k))
    for n in range(C // 256):
        at = slice(256 * n, 256 * (n + 1))
        b.gout[at, :] = dot(b.mixt[at, :], b.og[...].reshape(ND * T, F)).astype(BF)
    write(b.gout, g_out)
    total = b.lsum[1]
    for k in range(1, NY):
        loss_y(k).wait_recv()
        total = total + b.lrec[ND + k]
    b.lsum[2] = total
    go(loss_z())
    for c in range(NB):
        iz_copy(c).wait_recv()
        b.grad[CB * c: CB * (c + 1), :] += b.izrec[c].astype(F32)

    def k_lanes(j, own):
        return pl.ds(pl.multiple_of((zh if own else oz) * H + 128 * j, 128), 128)

    def k_z(j):
        at = b.vg.at[:, y, :, k_lanes(j, True)]
        return send(at, at, b.k_sem, j, zdev)

    def k_y(j, rel, which):
        at = b.vg.at[:, y, :, k_lanes(j, not which)]
        return send(at, at, b.k_sem, NJ + (2 * j + which) * NY + rel, ydev((y + rel) % NY))

    NJ = H // 128
    for j in range(H // 128):
        cols = slice(128 * j, 128 * (j + 1))
        g = b.grad[:, cols]
        gb = g.astype(BF)
        outs = [dot(b.wt[2 * j + e], gb) for e in (0, 1)]
        skips = jnp.where(low, b.skip[0, head0 + 2 * j], b.skip[0, head0 + 2 * j + 1])
        b.vg[:, y, :, lanes(j)] = (
            (jnp.where(low, outs[0], outs[1]) + skips * g).astype(BF).reshape(NA, CA, 128)
        )
        go(k_z(j))
        for rel in arrival(NY):
            go(k_y(j, rel, 0))
    dscore = jnp.zeros((T, T), F32)
    sums = []
    at_lane = lax.broadcasted_iota(jnp.int32, (T, 128), 1)
    rowcols = jnp.zeros((T, 128), F32)
    for j in range(H // 128):
        cols = slice(128 * j, 128 * (j + 1))
        g = b.grad[:, cols]
        gb = g.astype(BF)
        prod = g * b.pure[:, cols]
        for e in (0, 1):
            k = 2 * j + e
            here = low if e == 0 else jnp.logical_not(low)
            x = dot(gb, b.vmask[k], 1, 1)
            dscore = dscore + x * b.decay[k]
            sums.append(jnp.sum(x * b.both[k], axis=0, keepdims=True))
            rowcols = jnp.where(
                at_lane == k, jnp.sum(jnp.where(here, prod, 0.0), axis=1, keepdims=True), rowcols
            )
    dstep = jnp.concatenate(sums, axis=0)
    dcum = rowcols.T[:HH, :] - step * dstep
    ddecay = dot(dcum, causal.astype(F32), precision=HI)
    wrb = wr.astype(BF)
    draw = (dstep - rate * ddecay) * jax.nn.sigmoid(raw)
    drw = jnp.where(low, dot(dscore.T.astype(BF), wrb), dot(dscore.astype(BF), wrb)).T
    in_half = lax.broadcasted_iota(jnp.int32, (HB, T), 0) // HH == zh
    dsteps = jnp.where(in_half, jnp.concatenate([draw] * NZ, axis=0), 0.0)

    b.j1send[:W, :] = drw.astype(BF)
    b.j1send[W:, :] = dsteps.astype(BF)
    j1 = go(send(b.j1send, b.j1rec, b.iz_sem, NB, zdev))
    for j in range(NJ):
        k_z(j).wait_recv()
        for rel in arrival(NY):
            go(k_y(j, rel, 1))
    j1.wait_recv()
    b.j2send[:W, :] = (drw + b.j1rec[:W, :].astype(F32)).astype(BF)
    b.j2send[W:, :] = (dsteps + b.j1rec[W:, :].astype(F32)).astype(BF)
    b.j2rec[d] = b.j2send[...]

    def j2_copy(k):
        return send(b.j2send, b.j2rec.at[d], b.j2_sem, k, xdev((d + k) % ND))

    for k in arrival(ND):
        go(j2_copy(k))
    for k in arrival(ND):
        j2_copy(k).wait_recv()
    part = b.j2rec[0, :W, :].astype(F32)
    for q in range(1, ND):
        part = part + b.j2rec[q, :W, :].astype(F32)
    b.j3[y, :W, :] = part.astype(BF)
    for q in range(ND):
        b.j3[y, W + HB * q: W + HB * (q + 1), :] = b.j2rec[q, W:, :]

    def j3_copy(k):
        return send(b.j3.at[y], b.j3.at[y], b.j3_sem, k, ydev((y + k) % NY))

    for k in arrival(NY):
        go(j3_copy(k))
    loss_z().wait_recv()
    b.lout[...] = (
        jnp.zeros((8, 128), F32) + jnp.sum(b.lsum[2] + b.lrec[ND + NY]) / (T * ND * F * NY * NZ)
    )
    write(b.lout, loss)
    for j in range(NJ):
        for rel in arrival(NY):
            for which in (0, 1):
                k_y(j, rel, which).wait_recv()
        halves = [slice(h * H + 128 * j, h * H + 128 * (j + 1)) for h in range(NZ)]
        vg = jnp.concatenate([b.vg[:, :, :, at].reshape(ND * T, 128) for at in halves], axis=1)
        part = dot(b.srct[...], vg).astype(BF)
        for h, at in enumerate(halves):
            b.gin[:, at] = part[:, 128 * h: 128 * (h + 1)]
            write(b.gin.at[:, at], g_in.at[:, at])
    for k in arrival(NY):
        j3_copy(k).wait_recv()
    out = jnp.zeros((W + cfg.heads, F), F32)
    for q in range(NY):
        out = out + dot(b.j3[q], b.src[:, q].reshape(T, F))
    b.gside[...] = out.astype(BF)
    write(b.gside, g_side)

    finish()


def last(side, out, inn, loss, g_side, g_out, g_in, mean, sides, outs, inns, means, sems):
    moves = []
    for a, v, z in ((out, outs, g_out), (inn, inns, g_in), (side, sides, g_side)):
        n = a.shape[0]
        size = max(n // 4, 64)
        for i in range(n // size):
            moves.append((a, v, z, pl.ds(size * i, size)))
    fetch = [
        pltpu.make_async_copy(a.at[at], v.at[at], sems.at[0, i])
        for i, (a, v, z, at) in enumerate(moves)
    ]
    store = [
        pltpu.make_async_copy(v.at[at], z.at[0, at], sems.at[1, i])
        for i, (a, v, z, at) in enumerate(moves)
    ]
    whole = pltpu.make_async_copy(loss, means, sems.at[0, len(moves)])
    for cp in fetch + [whole]:
        cp.start()
    for f, z in zip(fetch, store):
        f.wait()
        z.start()
    whole.wait()
    mean[0] = jnp.max(means[...])
    for cp in store:
        cp.wait()


def local(states, final_state, retained, block_slot, w_in, w_side, w_out, a_rate, dt_bias, skip):
    nd, sec, nt = lax.axis_size("dp"), lax.axis_size("section"), lax.axis_size("tensor")
    ny = nt // NZ
    t, f = final_state.shape
    c = w_in.shape[2]
    heads = a_rate.shape[1]
    hb = c // P_SIZE
    sd = 2 * NS + heads
    sr = 2 * NS + hb
    h = c // NZ
    n = t * nd
    na, nb = min(CHUNKS[0], sec), CHUNKS[1]
    ca, cb = t // na, t // nb
    nstore = 3 + c // 128
    assert ny == nd and t == 128
    V, S = pltpu.VMEM, pltpu.SMEM

    def sems(k):
        return pltpu.SemaphoreType.DMA((2, k))

    scratch = dict(
        retained=S((sec,), jnp.int32), slot=S((sec,), jnp.int32),
        rate=S((1, heads), F32), bias=S((1, heads), F32), skip=S((1, heads), F32),
        layers0=V((2 * sec, t // sec, f // 2), BF), layers1=V((2 * sec, t // sec, f // 2), BF), stage=V((2, sec, t // sec, f), BF),
        src=V((na, nd, ca, f), BF), tgt=V((t, f), BF), final=V((t, f), BF), srct=V((f, n), BF),
        win=V((f, c + 2 * NS), BF), woutt=V((f, c), BF), wside=V((sd, f), BF), wout=V((c, f), BF), wstep=V((hb, f), BF),
        psend=V((na, ny, ca, c + 2 * NS), BF), prec=V((na, ny, ca, c + 2 * NS), BF),
        zsend=V((na, ca, h + 2 * NS), BF), zrec=V((na, ca, h + 2 * NS), BF),
        stsend=V((ny, hb, t), BF), strec=V((ny, hb, t), BF), stz=V((2, hb, t), BF),
        steps=V((hb, t), F32), rw=V((t, 2 * NS), F32), vals=V((t, h), F32), pure=V((t, h), F32),
        decay=V((hb // NZ, t, t), F32), both=V((hb // NZ, t, t), F32),
        wt=V((hb // NZ, t, t), BF), vmask=V((hb // NZ, t, t), BF), mix=V((nb, ny, cb, c), BF), mixt=V((c, n), BF),
        osend=V((nb, nd, cb, f), BF), orec=V((nb, nd, cb, f), BF), og=V((nb, nd, cb, f), BF),
        lsum=V((3, 8, 128), F32), lrec=V((nd + ny + 1, 8, 128), F32), lout=V((8, 128), F32),
        isend=V((nb, ny, cb, c), BF), irec=V((nb, ny, cb, c), BF),
        izsend=V((nb, cb, h), BF), izrec=V((nb, cb, h), BF), grad=V((t, h), F32),
        gout=V((c, f), BF), gin=V((f, c), BF), vg=V((na, ny, ca, c), BF),
        j1send=V((sr, t), BF), j1rec=V((sr, t), BF),
        j2send=V((sr, t), BF), j2rec=V((nd, sr, t), BF), j3=V((ny, sd, t), BF),
        gside=V((sd, f), BF),
        load_sem=pltpu.SemaphoreType.DMA((11,)), store_sem=pltpu.SemaphoreType.DMA((nstore,)),
        h1_sem=sems(2 * sec), h2_sem=sems(2 * sec), h3_sem=sems(sec), g_sem=sems(na * nd),
        c_sem=sems(na * ny), z_sem=sems(na), st_sem=sems(ny + 1), e_sem=sems(nb + 2 * nb * ny),
        f_sem=sems(nb * nd), h_sem=sems(nb * nd), i_sem=sems(nb * ny), iz_sem=sems(nb + 1),
        l_sem=sems(nd + ny + 1), k_sem=sems(h // 128 * (1 + 2 * ny)), j2_sem=sems(nd), j3_sem=sems(ny),
    )
    cfg = SimpleNamespace(
        names=tuple(scratch), nd=nd, sec=sec, ny=ny, t=t, f=f, c=c, hb=hb, heads=heads, na=na, nb=nb
    )
    hbm = pl.BlockSpec(memory_space=pl.ANY)
    shape = jax.ShapeDtypeStruct
    inn, side, out, loss = pl.pallas_call(
        functools.partial(kernel, cfg, None),
        out_shape=(
            shape((f, c), BF), shape((sd, f), BF), shape((c, f), BF), shape((8, 128), F32),
        ),
        in_specs=[hbm] * 10,
        out_specs=(hbm,) * 4,
        scratch_shapes=list(scratch.values()),
        compiler_params=pltpu.CompilerParams(
            collective_id=0, has_side_effects=True, vmem_limit_bytes=VMEM_BYTES
        ),
        name="distill",
    )(
        states, final_state, retained, block_slot, w_in, jnp.swapaxes(w_side, 1, 2), w_out,
        a_rate, dt_bias, skip,
    )
    g_side, g_out, g_in, mean = pl.pallas_call(
        last,
        out_shape=(
            shape((1, sd, f), BF), shape(w_out.shape, BF), shape(w_in.shape, BF), shape((1,), F32)
        ),
        in_specs=[hbm] * 4,
        out_specs=(hbm, hbm, hbm, pl.BlockSpec(memory_space=S)),
        scratch_shapes=[
            V((sd, f), BF), V((c, f), BF), V((f, c), BF), V((8, 128), F32),
            pltpu.SemaphoreType.DMA((2, 16)),
        ],
        compiler_params=pltpu.CompilerParams(vmem_limit_bytes=VMEM_BYTES),
        name="last",
    )(side, out, inn, loss)
    return g_in, jnp.swapaxes(g_side, 1, 2), g_out, mean


def solution(mesh):
    placed = (
        P("section", "dp", "tensor"),
        P("dp", "tensor"),
        P(),
        P(),
        P("section", "tensor", "dp"),
        P("section", "tensor", None),
        P("section", "dp", "tensor"),
        P("section", None),
        P("section", None),
        P("section", None),
    )
    return jax.shard_map(
        local,
        mesh=mesh,
        in_specs=placed,
        out_specs=(
            P("section", "tensor", "dp"),
            P("section", "tensor", None),
            P("section", "dp", "tensor"),
            P("section"),
        ),
        check_vma=False,
    )
```
